256 devices in a mesh: ci: 8 (over z), co: 16 (over y, x_hi, core), sp: 2 (over x_lo).
Axes of the slice: x: 4 (x_hi: 2, x_lo: 2; x = x_hi * 2 + x_lo), y: 4, z: 8, core: 2. Of those that a mesh axis runs over, the one named last changes fastest.
Arguments:
- features: bfloat16 [32, 512, 256], P(None, 'ci', 'sp'), may hold values from -6 to 6
- weight: bfloat16 [27, 512, 512], P(None, 'ci', 'co'), may hold values from -0.0546875 to 0.0546875
- bias_vector: float32 [512], P('co'), may hold values from -3 to 3
- cotangent: bfloat16 [32, 512, 256], P('ci', 'co', 'sp'), may hold values from -6 to 6
Outputs:
- activated: bfloat16 [32, 512, 256], P('ci', 'co', 'sp')
- input_grad: float32 [32, 512, 256], P('co', 'ci', 'sp')
- weight_grad: float32 [27, 512, 512], P(None, 'ci', 'co')
- bias_grad: float32 [512], P('co')
The draws below stay inside these ranges and needn't reach their ends.
All inputs are finite; a program needn't handle non-finite values.
Results may differ from the reference program's by a relative error of at most 0.02.
Values may be sent and summed in bfloat16 or wider, within the bound.
No kernel may reach another device: no remote copies, remote signals or barrier semaphores. Data moves between devices by JAX's collectives and lax.ppermute only.
A program may use at most 64 MiB of HBM per device.

```python
import jax
import jax.numpy as jnp
from jax import lax

C = 512
SY = 32
SZ = 32
SX = 8
N_CI = 8


def levels(key, extent, cuts, least, high):
    def one(axis_at, blocks):
        draws = jax.random.uniform(jax.random.fold_in(jax.random.fold_in(key, 6), axis_at), (blocks,), jnp.float32, least / len(cuts), high / len(cuts))
        return jnp.repeat(jnp.exp(draws), extent[axis_at] // blocks).reshape((-1,) + (1,) * (len(extent) - axis_at - 1))

    gain = one(*cuts[0])
    for cut in cuts[1:]:
        gain = gain * one(*cut)
    return gain


def gaussian(rng, dims, deviation, bound, split=(), dtype=jnp.bfloat16):
    drawn = jax.random.normal(rng, dims, jnp.float32) * deviation
    if len(split) > 0:
        drawn = levels(rng, dims, split, -0.22, 0.18) * drawn
    return jnp.clip(drawn, min=-bound, max=bound).astype(dtype)


def setup_inputs(seed: int = 0) -> dict:
    key_list = jax.random.split(jax.random.key(seed), 5)
    features = gaussian(key_list[0], (SY, C, SX * SZ), 1.0, 6.0, ((1, 8), (2, 2)))
    weight = gaussian(key_list[1], (27, C, C), (27 * C) ** -0.5, 0.0546875, ((1, 8), (2, 16)))
    bias_vector = gaussian(key_list[2], (C,), 0.5, 3.0, ((0, 16),), jnp.float32)
    cotangent = gaussian(key_list[3], (SY, C, SX * SZ), 1.0, 6.0, ((0, 8), (1, 16), (2, 2)))
    return dict(features=features, weight=weight, bias_vector=bias_vector, cotangent=cotangent)


FORWARD_DIMS = ('NDHWC', 'DHWIO', 'NDHWC')
BACKWARD_DIMS = ('NDHWC', 'DHWOI', 'NDHWC')

def smooth(values):
    return jax.nn.gelu(values, approximate=True)

def correlate(volume, kernel, numbers):
    return lax.conv_general_dilated(volume[None], kernel, (1, 1, 1), ((1, 1), (1, 1), (1, 1)), dimension_numbers=numbers, precision=lax.Precision.HIGHEST)[0]

def to_volume(array):
    return array.reshape(SY, C, SX, SZ).transpose(0, 2, 3, 1)

def from_volume(array):
    return array.transpose(0, 3, 1, 2).reshape(SY, C, SX * SZ)

def reference(features, weight, bias_vector, cotangent):
    kernel = weight.astype(jnp.float32).reshape(3, 3, 3, C, C)
    inputs = to_volume(features).astype(jnp.float32)
    width_in = C // N_CI
    summed = jnp.zeros((SY, SX, SZ, C), jnp.float32)
    for block_index in range(N_CI):
        lower_edge = block_index * width_in
        partial_term = correlate(inputs[..., lower_edge:lower_edge + width_in], kernel[:, :, :, lower_edge:lower_edge + width_in, :], FORWARD_DIMS)
        rounded = lax.optimization_barrier(partial_term.astype(jnp.bfloat16))
        summed = summed + rounded.astype(jnp.float32)
    preact = summed + bias_vector
    activated = smooth(preact).astype(jnp.bfloat16)
    unused, pullback = jax.vjp(smooth, preact)
    grad_pre = pullback(to_volume(cotangent).astype(jnp.float32))[0].astype(jnp.bfloat16)
    grad_wide = grad_pre.astype(jnp.float32)
    bias_grad = lax.optimization_barrier(jnp.sum(grad_wide, axis=(0, 1, 2)))
    padded = jnp.pad(inputs, ((1, 1), (1, 1), (1, 1), (0, 0)))
    rows_flat = grad_wide.reshape(-1, C)
    pieces = []
    for tap_index in range(27):
        depth_y = tap_index // 9
        depth_x = tap_index // 3 % 3
        depth_z = tap_index % 3
        shifted = padded[depth_y:depth_y + SY, depth_x:depth_x + SX, depth_z:depth_z + SZ].reshape(-1, C)
        pieces.append(lax.dot_general(shifted, rows_flat, (((0,), (0,)), ((), ())), precision=lax.Precision.HIGHEST))
    weight_grad = jnp.stack(pieces)
    flipped = kernel[::-1, ::-1, ::-1]
    input_grad = correlate(grad_wide, flipped, BACKWARD_DIMS)
    return (from_volume(activated), from_volume(input_grad), weight_grad, bias_grad)
```

```python
import jax
import jax.numpy as jnp
from jax import lax
from jax.experimental import pallas as pl
from jax.experimental.pallas import tpu as pltpu
from jax.sharding import PartitionSpec as P

SZ = 32
LANES = 128
BF16 = jnp.bfloat16
F32 = jnp.float32
VMEM = pl.BlockSpec(memory_space=pltpu.VMEM)
SMEM = pl.BlockSpec(memory_space=pltpu.SMEM)


def call(body, outs, specs, flops, moved, scratch=()):
    return pl.pallas_call(
        body,
        out_shape=outs,
        in_specs=specs,
        out_specs=jax.tree.map(lambda _: VMEM, outs),
        scratch_shapes=list(scratch),
        cost_estimate=pl.CostEstimate(flops=flops, bytes_accessed=moved, transcendentals=0),
        compiler_params=pltpu.CompilerParams(vmem_limit_bytes=40 * 2**20),
    )


def lane(shape):
    return lax.broadcasted_iota(jnp.int32, shape, len(shape) - 1)


def pack_plane(side, planes):
    packed = None
    at = lane(planes[0].shape)
    for k, plane in enumerate(planes):
        moved = pltpu.roll(plane, lax.rem(SZ * k + SZ * (1 - side), LANES), 1)
        packed = moved if packed is None else jnp.where(at >= SZ * k, moved, packed)
    return packed


def neighbours(own, low, high, k):
    at = lane(own.shape)
    before = jnp.where(at < SZ, pltpu.roll(low, (-SZ * k) % LANES, 1), pltpu.roll(own, SZ, 1))
    after = jnp.where(
        at >= LANES - SZ,
        pltpu.roll(high, (LANES - SZ - SZ * k) % LANES, 1),
        pltpu.roll(own, LANES - SZ, 1),
    )
    return before, own, after


def split_halo(side, packed):
    zero = jnp.zeros_like(packed)
    return jnp.where(side == 1, packed, zero), jnp.where(side == 0, packed, zero)


def along_z(terms):
    lower, middle, upper = terms
    width = middle.shape[1]
    z = lane((middle.shape[0], LANES)) % SZ
    parts = []
    for start in range(0, width, LANES):
        cut = slice(start, start + LANES)
        parts.append(
            middle[:, cut]
            + jnp.where(z == 0, 0.0, pltpu.roll(lower[:, cut], 1, 1))
            + jnp.where(z == SZ - 1, 0.0, pltpu.roll(upper[:, cut], LANES - 1, 1))
        )
    return parts


def pack_features(side_ref, features_ref, out_ref):
    side = side_ref[0]
    for group in range(out_ref.shape[0]):
        out_ref[group] = pack_plane(side, [features_ref[4 * group + k] for k in range(4)])


def correlate(taps_ref, spread_ref, rows_y, width, store):
    depth = 3 * spread_ref.shape[1]
    taps = taps_ref[...]
    for y in range(0, rows_y, 2):
        columns = jnp.concatenate(
            [spread_ref[y + k : y + k + 3].reshape(depth, LANES) for k in range(2)], axis=1
        )
        product = jnp.dot(taps, columns, preferred_element_type=F32)
        parts = along_z([product[c * width : (c + 1) * width] for c in range(3)])
        for k in range(2):
            store(y + k, parts[k].astype(BF16))


def forward(side_ref, features_ref, halo_ref, weight_ref, out_ref, spread_ref, taps_ref):
    rows_y, width_in, _ = features_ref.shape
    width_out = weight_ref.shape[1]
    side = side_ref[0]
    blank = jnp.zeros(spread_ref.shape[1:], BF16)
    spread_ref[0] = blank
    spread_ref[rows_y + 1] = blank
    for group in range(rows_y // 4):
        low, high = split_halo(side, halo_ref[group])
        for k in range(4):
            y = 4 * group + k
            seen = neighbours(features_ref[y], low, high, k)
            for b in range(3):
                spread_ref[y + 1, b * width_in : (b + 1) * width_in] = seen[b]
    for c in range(3):
        taps_ref[c * width_out : (c + 1) * width_out] = jnp.concatenate(
            [weight_ref[3 * ab + c] for ab in range(9)], axis=1
        )

    def store(y, value):
        out_ref[y] = value

    correlate(taps_ref, spread_ref, rows_y, width_out, store)


def pointwise(side_ref, partial_ref, bias_ref, cotangent_ref, act_ref, grad_ref, edge_ref):
    total = partial_ref[0].astype(F32)
    for k in range(1, partial_ref.shape[0]):
        total = total + partial_ref[k].astype(F32)
    pre = total + bias_ref[...][None]
    scale, cubic = 0.7978845608, 0.044715
    square = pre * pre
    bend = jnp.tanh(scale * (pre + cubic * (square * pre)))
    half = 0.5 * (1.0 + bend)
    act_ref[...] = (pre * half).astype(BF16)
    slope = half + 0.5 * pre * (1.0 - bend * bend) * (scale * (1.0 + 3.0 * cubic * square))
    grad = (cotangent_ref[...].astype(F32) * slope).astype(BF16)
    grad_ref[...] = grad
    edge_ref[...] = pack_plane(side_ref[0], [grad[k] for k in range(4)])


def replicate(grad_ref, halo_ref, out_ref):
    rows = grad_ref.shape[0] * grad_ref.shape[1]
    own = grad_ref[...].reshape(rows, LANES)
    for k in range(out_ref.shape[0]):
        out_ref[k, :rows] = own
        out_ref[k, rows:] = halo_ref[...]


def spread_gradient(side, gathered_ref, width, put):
    rows = 4 * width
    for group in range(gathered_ref.shape[0]):
        low, high = split_halo(side, gathered_ref[group, rows:])
        for k in range(4):
            own = gathered_ref[group, k * width : (k + 1) * width]
            put(4 * group + k, neighbours(own, low, high, k))


def backward(side_ref, gathered_ref, weight_ref, out_ref, spread_ref, taps_ref):
    rows_y, width_in, _ = out_ref.shape
    width_out = weight_ref.shape[1]
    blank = jnp.zeros(spread_ref.shape[1:], BF16)
    spread_ref[0] = blank
    spread_ref[rows_y + 1] = blank

    def put(y, seen):
        for b in range(3):
            spread_ref[y + 1, b * width_out : (b + 1) * width_out] = seen[b]

    spread_gradient(side_ref[0], gathered_ref, width_out, put)
    for c in range(3):
        block = jnp.concatenate([weight_ref[26 - 3 * ab - c] for ab in range(9)], axis=0)
        taps_ref[c * width_in : (c + 1) * width_in] = block.T

    def store(y, value):
        out_ref[y] = value

    correlate(taps_ref, spread_ref, rows_y, width_in, store)


def filter_gradient(side_ref, features_ref, gathered_ref, out_ref, grad_ref, rows_ref):
    rows_y, width_in, _ = features_ref.shape
    width_out = grad_ref.shape[0] // 9
    z = lane((width_out, LANES)) % SZ
    zero = jnp.zeros((width_out, LANES), BF16)

    def put(y, seen):
        columns = slice(y * LANES, (y + 1) * LANES)
        for b in range(3):
            own = seen[2 - b]
            moved = (
                jnp.where(z == SZ - 1, zero, pltpu.roll(own, LANES - 1, 1)),
                own,
                jnp.where(z == 0, zero, pltpu.roll(own, 1, 1)),
            )
            for c in range(3):
                start = (3 * b + c) * width_out
                grad_ref[start : start + width_out, columns] = moved[c]

    spread_gradient(side_ref[0], gathered_ref, width_out, put)
    for a in range(3):
        for y in range(rows_y):
            source = y + a - 1
            inside = 0 <= source < rows_y
            rows_ref[a * width_in : (a + 1) * width_in, y * LANES : (y + 1) * LANES] = (
                features_ref[source] if inside else jnp.zeros((width_in, LANES), BF16)
            )
    over_voxels = (((1,), (1,)), ((), ()))
    grads = grad_ref[...]
    total = lax.dot_general(grads, rows_ref[...], over_voxels, preferred_element_type=F32)
    middle = 4 * width_out
    ones = jnp.ones((16, grads.shape[1]), BF16)
    bias = lax.dot_general(
        ones, grad_ref[middle : middle + width_out], over_voxels, preferred_element_type=F32
    )
    count = total.shape[0]
    rounded = total.astype(BF16)
    out_ref[:count] = rounded[:, : 2 * width_in]
    last = rounded[:, 2 * width_in :]
    out_ref[count : count + count // 2] = jnp.concatenate(
        [last[: count // 2], last[count // 2 :]], axis=1
    )
    high = bias.astype(BF16)
    rest = bias - high.astype(F32)
    mid = rest.astype(BF16)
    low = (rest - mid.astype(F32)).astype(BF16)
    row = lax.broadcasted_iota(jnp.int32, bias.shape, 0)
    nothing = jnp.zeros_like(bias)
    terms = jnp.where(
        row == 0,
        high.astype(F32),
        jnp.where(row == 1, mid.astype(F32), jnp.where(row == 2, low.astype(F32), nothing)),
    ).astype(BF16)
    out_ref[count + count // 2 :] = jnp.concatenate(
        [terms, jnp.zeros((16, LANES - width_out), BF16)], axis=1
    )


def finish_filter(own_ref, other_ref, weight_ref, bias_ref):
    _, width_out, width_in = weight_ref.shape
    count = 9 * width_out
    half = count // 2
    both = own_ref[...].astype(F32) + other_ref[...].astype(F32)
    for bc in range(9):
        rows = slice(bc * width_out, (bc + 1) * width_out)
        first = both[rows]
        weight_ref[bc] = first[:, :width_in]
        weight_ref[9 + bc] = first[:, width_in:]
        for step in range(0, width_out, 16):
            start = bc * width_out + step
            if start < half:
                piece = both[count + start : count + start + 16, :width_in]
            else:
                start -= half
                piece = both[count + start : count + start + 16, width_in:]
            weight_ref[18 + bc, step : step + 16] = piece
    first = count + half
    mine = own_ref[first:].astype(F32)
    theirs = other_ref[first:].astype(F32)
    bias_ref[...] = (
        jnp.sum(mine, axis=0, keepdims=True) + jnp.sum(theirs, axis=0, keepdims=True)
    )[:, :width_out]


def add_shares(shares_ref, out_ref):
    total = shares_ref[0].astype(F32)
    for k in range(1, shares_ref.shape[0]):
        total = total + shares_ref[k].astype(F32)
    out_ref[...] = total


def local(features, weight, bias_vector, cotangent):
    rows_y, width_in, _ = features.shape
    width_out = weight.shape[2]
    n_ci, n_co = lax.axis_size("ci"), lax.axis_size("co")
    shape = jax.ShapeDtypeStruct
    side = lax.axis_index("sp").astype(jnp.int32).reshape(1)
    swap = [(0, 1), (1, 0)]
    taps = weight.transpose(0, 2, 1)
    work = 2 * 27 * rows_y * LANES * width_in * width_out
    size = rows_y * LANES * 2

    edge = call(
        pack_features,
        shape((rows_y // 4, width_in, LANES), BF16),
        [SMEM, VMEM],
        0,
        2 * size * width_in,
    )(side, features)
    halo = lax.ppermute(edge, "sp", swap)
    partial = call(
        forward,
        shape((rows_y, width_out, LANES), BF16),
        [SMEM, VMEM, VMEM, VMEM],
        work,
        size * (width_in + width_out),
        [
            pltpu.VMEM((rows_y + 2, 3 * width_in, LANES), BF16),
            pltpu.VMEM((3 * width_out, 9 * width_in), BF16),
        ],
    )(side, features, halo, taps)
    shares = lax.all_to_all(
        partial.reshape(n_ci, rows_y // n_ci, width_out, LANES), "ci", 0, 0, tiled=True
    )
    block = (rows_y // n_ci, width_out, LANES)
    activated, grad_pre, edge = call(
        pointwise,
        (shape(block, BF16), shape(block, BF16), shape((width_out, LANES), BF16)),
        [SMEM, VMEM, VMEM, VMEM],
        0,
        2 * size * width_out,
    )(side, shares, bias_vector.reshape(width_out, 1), cotangent)
    halo = lax.ppermute(edge, "sp", swap)
    rows = 5 * width_out
    copies = call(
        replicate, shape((n_ci, rows, LANES), BF16), [VMEM, VMEM], 0, 2 * size * width_out
    )(grad_pre, halo)
    gathered = lax.all_to_all(copies, "ci", 0, 0, tiled=True)
    shares = call(
        backward,
        shape((rows_y, width_in, LANES), BF16),
        [SMEM, VMEM, VMEM],
        work,
        size * (width_in + width_out),
        [
            pltpu.VMEM((rows_y + 2, 3 * width_out, LANES), BF16),
            pltpu.VMEM((3 * width_in, 9 * width_out), BF16),
        ],
    )(side, gathered, taps)
    shares = lax.all_to_all(
        shares.reshape(n_co, rows_y // n_co, width_in, LANES), "co", 0, 0, tiled=True
    )
    packed = call(
        filter_gradient,
        shape((9 * width_out + 9 * width_out // 2 + 16, LANES), BF16),
        [SMEM, VMEM, VMEM],
        work,
        size * (width_in + width_out),
        [
            pltpu.VMEM((9 * width_out, rows_y * LANES), BF16),
            pltpu.VMEM((3 * width_in, rows_y * LANES), BF16),
        ],
    )(side, features, gathered)
    other = lax.ppermute(packed, "sp", swap)
    input_grad = call(
        add_shares,
        shape((rows_y // n_co, width_in, LANES), F32),
        [VMEM],
        0,
        size * width_in,
    )(shares)
    weight_grad, bias_grad = call(
        finish_filter,
        (shape((27, width_out, width_in), F32), shape((1, width_out), F32)),
        [VMEM, VMEM],
        0,
        27 * 4 * width_in * width_out,
    )(packed, other)
    return (activated, input_grad, weight_grad.transpose(0, 2, 1), bias_grad.reshape(width_out))


def solution(mesh):
    placed = (P(None, "ci", "sp"), P(None, "ci", "co"), P("co"), P("ci", "co", "sp"))
    return jax.shard_map(
        local,
        mesh=mesh,
        in_specs=placed,
        out_specs=(P("ci", "co", "sp"), P("co", "ci", "sp"), P(None, "ci", "co"), P("co")),
        check_vma=False,
    )
```

```python
import jax
import jax.numpy as jnp
from jax import lax
from jax.experimental import pallas as pl
from jax.experimental.pallas import tpu as pltpu
from jax.sharding import PartitionSpec as P

SZ = 32
LANES = 128
BF16 = jnp.bfloat16
F32 = jnp.float32
VMEM = pl.BlockSpec(memory_space=pltpu.VMEM)
SMEM = pl.BlockSpec(memory_space=pltpu.SMEM)
HBM = pl.BlockSpec(memory_space=pltpu.HBM)


def call(body, outs, specs, flops, moved, scratch=()):
    return pl.pallas_call(
        body,
        out_shape=outs,
        in_specs=specs,
        out_specs=jax.tree.map(lambda _: VMEM, outs),
        scratch_shapes=list(scratch),
        cost_estimate=pl.CostEstimate(flops=flops, bytes_accessed=moved, transcendentals=0),
        compiler_params=pltpu.CompilerParams(vmem_limit_bytes=40 * 2**20),
    )


def lane(shape):
    return lax.broadcasted_iota(jnp.int32, shape, len(shape) - 1)


def pack_plane(side, planes):
    packed = None
    at = lane(planes[0].shape)
    for k, plane in enumerate(planes):
        moved = pltpu.roll(plane, lax.rem(SZ * k + SZ * (1 - side), LANES), 1)
        packed = moved if packed is None else jnp.where(at >= SZ * k, moved, packed)
    return packed


def neighbours(own, low=None, high=None, k=0):
    at = lane(own.shape)
    zero = jnp.zeros_like(own)
    left = zero if low is None else pltpu.roll(low, (-SZ * k) % LANES, 1)
    right = zero if high is None else pltpu.roll(high, (LANES - SZ - SZ * k) % LANES, 1)
    before = jnp.where(at < SZ, left, pltpu.roll(own, SZ, 1))
    after = jnp.where(at >= LANES - SZ, right, pltpu.roll(own, LANES - SZ, 1))
    return before, own, after


def split_halo(side, packed):
    zero = jnp.zeros_like(packed)
    return jnp.where(side == 1, packed, zero), jnp.where(side == 0, packed, zero)


def along_z(terms):
    lower, middle, upper = terms
    width = middle.shape[1]
    z = lane((middle.shape[0], LANES)) % SZ
    parts = []
    for start in range(0, width, LANES):
        cut = slice(start, start + LANES)
        parts.append(
            middle[:, cut]
            + jnp.where(z == 0, 0.0, pltpu.roll(lower[:, cut], 1, 1))
            + jnp.where(z == SZ - 1, 0.0, pltpu.roll(upper[:, cut], LANES - 1, 1))
        )
    return parts


def correlate_rows(taps, spread_ref, y, width, store):
    depth = 3 * spread_ref.shape[1]
    columns = jnp.concatenate(
        [spread_ref[y + k : y + k + 3].reshape(depth, LANES) for k in range(2)], axis=1
    )
    product = jnp.dot(taps, columns, preferred_element_type=F32)
    parts = along_z([product[c * width : (c + 1) * width] for c in range(3)])
    for k in range(2):
        store(y + k, parts[k].astype(BF16))


def forward(
    side_ref, features_hbm, weight_hbm, out_ref,
    features_ref, weight_ref, spread_ref, taps_ref, edge_taps_ref, edge_ref, sems,
):
    rows_y, width_in, _ = features_ref.shape
    width_out = weight_ref.shape[1]
    groups = rows_y // 4
    pieces = sems.shape[0] - 1
    step = rows_y // pieces
    fetch = [
        pltpu.make_async_copy(
            features_hbm.at[pl.ds(k * step, step)], features_ref.at[pl.ds(k * step, step)], sems.at[k]
        )
        for k in range(pieces)
    ]
    fetch_weight = pltpu.make_async_copy(weight_hbm, weight_ref, sems.at[pieces])
    fetch[0].start()
    fetch_weight.start()
    for copy in fetch[1:]:
        copy.start()
    side = side_ref[0]
    blank = jnp.zeros(spread_ref.shape[1:], BF16)
    spread_ref[0] = blank
    spread_ref[rows_y + 1] = blank
    fetch_weight.wait()
    for c in range(3):
        rows = slice(c * width_out, (c + 1) * width_out)
        taps_ref[rows] = jnp.concatenate([weight_ref[3 * ab + c] for ab in range(9)], axis=1)
        edge_taps_ref[rows] = jnp.concatenate(
            [weight_ref[9 * a + c + 6 * side] for a in range(3)], axis=1
        )
    taps = taps_ref[...]

    def store(y, value):
        start = y % 4 * width_out
        out_ref[y // 4, start : start + width_out] = value

    done = 0
    for group in range(groups):
        if group * 4 % step == 0:
            fetch[group * 4 // step].wait()
        planes = [features_ref[4 * group + k] for k in range(4)]
        for k in range(4):
            seen = neighbours(planes[k])
            for b in range(3):
                spread_ref[4 * group + k + 1, b * width_in : (b + 1) * width_in] = seen[b]
        edge_ref[group + 1] = pack_plane(side, planes)
        while done + 2 < 4 * group + 4 or (group == groups - 1 and done < rows_y):
            correlate_rows(taps, spread_ref, done, width_out, store)
            done += 2
    none = jnp.zeros(edge_ref.shape[1:], BF16)
    edge_ref[0] = none
    edge_ref[groups + 1] = none
    at = lane((width_in, LANES))
    columns = []
    for group in range(groups):
        last, here, following = (edge_ref[group + k] for k in range(3))
        above = jnp.where(at < SZ, pltpu.roll(last, SZ, 1), pltpu.roll(here, SZ, 1))
        below = jnp.where(
            at >= LANES - SZ,
            pltpu.roll(following, LANES - SZ, 1),
            pltpu.roll(here, LANES - SZ, 1),
        )
        columns.append(jnp.concatenate([above, here, below], axis=0))
    product = jnp.dot(
        edge_taps_ref[...], jnp.concatenate(columns, axis=1), preferred_element_type=F32
    )
    parts = along_z([product[c * width_out : (c + 1) * width_out] for c in range(3)])
    for group in range(groups):
        out_ref[group, 4 * width_out :] = parts[group].astype(BF16)


def reduce_rows(side_ref, shares_ref, cotangent_ref, own_ref, message_ref):
    total = shares_ref[0].astype(F32)
    for k in range(1, shares_ref.shape[0]):
        total = total + shares_ref[k].astype(F32)
    rows, width, _ = cotangent_ref.shape
    planes = [total[k * width : (k + 1) * width] for k in range(rows)]
    for k in range(rows):
        own_ref[k] = planes[k]
    side = side_ref[0]
    message_ref[0] = total[rows * width :]
    message_ref[1] = pack_plane(side, planes)
    message_ref[2] = pack_plane(side, [cotangent_ref[k].astype(F32) for k in range(rows)])


def gelu(pre, cotangent):
    scale, cubic = 0.7978845608, 0.044715
    square = pre * pre
    bend = jnp.tanh(scale * (pre + cubic * (square * pre)))
    half = 0.5 * (1.0 + bend)
    slope = half + 0.5 * pre * (1.0 - bend * bend) * (scale * (1.0 + 3.0 * cubic * square))
    return (pre * half).astype(BF16), (cotangent * slope).astype(BF16)


def pointwise(side_ref, own_ref, mine_ref, theirs_ref, bias_ref, cotangent_ref, act_ref, out_ref):
    rows, width, _ = own_ref.shape
    side = side_ref[0]
    bias = jnp.broadcast_to(bias_ref[...], (width, LANES))
    at = lane((width, LANES))
    edge = at // SZ == 3 * (1 - side)
    added = theirs_ref[0]
    grads = []
    for k in range(rows):
        moved = pltpu.roll(added, lax.rem(3 * SZ * (1 - side) - SZ * k + LANES, LANES), 1)
        pre = own_ref[k] + jnp.where(edge, moved, 0.0) + bias
        act, grad = gelu(pre, cotangent_ref[k].astype(F32))
        act_ref[k] = act
        grads.append(grad)
    _, grad = gelu(theirs_ref[1] + mine_ref[0] + bias, theirs_ref[2])
    block = jnp.concatenate(grads + [grad], axis=0)
    for k in range(out_ref.shape[0]):
        out_ref[k] = block


def spread_gradient(side, gathered_ref, width, put):
    rows = 4 * width
    for group in range(gathered_ref.shape[0]):
        low, high = split_halo(side, gathered_ref[group, rows:])
        for k in range(4):
            own = gathered_ref[group, k * width : (k + 1) * width]
            put(4 * group + k, neighbours(own, low, high, k))


def backward(side_ref, gathered_ref, weight_ref, out_ref, spread_ref, taps_ref):
    rows_y, width_in, _ = out_ref.shape
    width_out = weight_ref.shape[1]
    blank = jnp.zeros(spread_ref.shape[1:], BF16)
    spread_ref[0] = blank
    spread_ref[rows_y + 1] = blank

    def put(y, seen):
        for b in range(3):
            spread_ref[y + 1, b * width_out : (b + 1) * width_out] = seen[b]

    spread_gradient(side_ref[0], gathered_ref, width_out, put)
    for c in range(3):
        block = jnp.concatenate([weight_ref[26 - 3 * ab - c] for ab in range(9)], axis=0)
        taps_ref[c * width_in : (c + 1) * width_in] = block.T

    def store(y, value):
        out_ref[y] = value

    taps = taps_ref[...]
    for y in range(0, rows_y, 2):
        correlate_rows(taps, spread_ref, y, width_in, store)


def filter_gradient(side_ref, features_ref, gathered_ref, out_ref, grad_ref, rows_ref):
    rows_y, width_in, _ = features_ref.shape
    width_out = grad_ref.shape[0] // 9
    z = lane((width_out, LANES)) % SZ
    zero = jnp.zeros((width_out, LANES), BF16)

    def put(y, seen):
        columns = slice(y * LANES, (y + 1) * LANES)
        for b in range(3):
            own = seen[2 - b]
            moved = (
                jnp.where(z == SZ - 1, zero, pltpu.roll(own, LANES - 1, 1)),
                own,
                jnp.where(z == 0, zero, pltpu.roll(own, 1, 1)),
            )
            for c in range(3):
                start = (3 * b + c) * width_out
                grad_ref[start : start + width_out, columns] = moved[c]

    spread_gradient(side_ref[0], gathered_ref, width_out, put)
    for a in range(3):
        for y in range(rows_y):
            source = y + a - 1
            inside = 0 <= source < rows_y
            rows_ref[a * width_in : (a + 1) * width_in, y * LANES : (y + 1) * LANES] = (
                features_ref[source] if inside else jnp.zeros((width_in, LANES), BF16)
            )
    over_voxels = (((1,), (1,)), ((), ()))
    grads = grad_ref[...]
    total = lax.dot_general(grads, rows_ref[...], over_voxels, preferred_element_type=F32)
    middle = 4 * width_out
    ones = jnp.ones((16, grads.shape[1]), BF16)
    bias = lax.dot_general(
        ones, grad_ref[middle : middle + width_out], over_voxels, preferred_element_type=F32
    )
    count = total.shape[0]
    rounded = total.astype(BF16)
    out_ref[:count] = rounded[:, : 2 * width_in]
    last = rounded[:, 2 * width_in :]
    out_ref[count : count + count // 2] = jnp.concatenate(
        [last[: count // 2], last[count // 2 :]], axis=1
    )
    high = bias.astype(BF16)
    rest = bias - high.astype(F32)
    mid = rest.astype(BF16)
    low = (rest - mid.astype(F32)).astype(BF16)
    row = lax.broadcasted_iota(jnp.int32, bias.shape, 0)
    nothing = jnp.zeros_like(bias)
    terms = jnp.where(
        row == 0,
        high.astype(F32),
        jnp.where(row == 1, mid.astype(F32), jnp.where(row == 2, low.astype(F32), nothing)),
    ).astype(BF16)
    out_ref[count + count // 2 :] = jnp.concatenate(
        [terms, jnp.zeros((16, LANES - width_out), BF16)], axis=1
    )


def finish_filter(own_ref, other_ref, weight_ref, bias_ref):
    _, width_out, width_in = weight_ref.shape
    count = 9 * width_out
    half = count // 2
    both = own_ref[...].astype(F32) + other_ref[...].astype(F32)
    for bc in range(9):
        rows = slice(bc * width_out, (bc + 1) * width_out)
        first = both[rows]
        weight_ref[bc] = first[:, :width_in]
        weight_ref[9 + bc] = first[:, width_in:]
        for step in range(0, width_out, 16):
            start = bc * width_out + step
            if start < half:
                piece = both[count + start : count + start + 16, :width_in]
            else:
                start -= half
                piece = both[count + start : count + start + 16, width_in:]
            weight_ref[18 + bc, step : step + 16] = piece
    first = count + half
    mine = own_ref[first:].astype(F32)
    theirs = other_ref[first:].astype(F32)
    bias_ref[...] = (
        jnp.sum(mine, axis=0, keepdims=True) + jnp.sum(theirs, axis=0, keepdims=True)
    )[:, :width_out]


def add_shares(shares_ref, out_ref):
    total = shares_ref[0].astype(F32)
    for k in range(1, shares_ref.shape[0]):
        total = total + shares_ref[k].astype(F32)
    out_ref[...] = total


def local(features, weight, bias_vector, cotangent):
    rows_y, width_in, _ = features.shape
    width_out = weight.shape[2]
    n_ci, n_co = lax.axis_size("ci"), lax.axis_size("co")
    shape = jax.ShapeDtypeStruct
    side = lax.axis_index("sp").astype(jnp.int32).reshape(1)
    swap = [(0, 1), (1, 0)]
    taps = weight.transpose(0, 2, 1)
    work = 2 * 27 * rows_y * LANES * width_in * width_out
    size = rows_y * LANES * 2

    block = 5 * width_out
    partial = call(
        forward,
        shape((n_ci, block, LANES), BF16),
        [SMEM, HBM, HBM],
        work,
        size * (width_in + width_out),
        [
            pltpu.VMEM(features.shape, BF16),
            pltpu.VMEM(taps.shape, BF16),
            pltpu.VMEM((rows_y + 2, 3 * width_in, LANES), BF16),
            pltpu.VMEM((3 * width_out, 9 * width_in), BF16),
            pltpu.VMEM((3 * width_out, 3 * width_in), BF16),
            pltpu.VMEM((rows_y // 4 + 2, width_in, LANES), BF16),
            pltpu.SemaphoreType.DMA((5,)),
        ],
    )(side, features, taps)
    shares = lax.all_to_all(partial, "ci", 0, 0, tiled=True)
    own, mine = call(
        reduce_rows,
        (shape(cotangent.shape, F32), shape((3, width_out, LANES), F32)),
        [SMEM, VMEM, VMEM],
        0,
        2 * size * width_out,
    )(side, shares, cotangent)
    theirs = lax.ppermute(mine, "sp", swap)
    activated, copies = call(
        pointwise,
        (shape(cotangent.shape, BF16), shape((n_ci, block, LANES), BF16)),
        [SMEM, VMEM, VMEM, VMEM, VMEM, VMEM],
        0,
        2 * size * width_out,
    )(side, own, mine, theirs, bias_vector.reshape(width_out, 1), cotangent)
    gathered = lax.all_to_all(copies, "ci", 0, 0, tiled=True)
    packed = call(
        filter_gradient,
        shape((9 * width_out + 9 * width_out // 2 + 16, LANES), BF16),
        [SMEM, VMEM, VMEM],
        work,
        size * (width_in + width_out),
        [
            pltpu.VMEM((9 * width_out, rows_y * LANES), BF16),
            pltpu.VMEM((3 * width_in, rows_y * LANES), BF16),
        ],
    )(side, features, gathered)
    other = lax.ppermute(packed, "sp", swap)
    gathered, packed = lax.optimization_barrier((gathered, packed))
    shares = call(
        backward,
        shape((rows_y, width_in, LANES), BF16),
        [SMEM, VMEM, VMEM],
        work,
        size * (width_in + width_out),
        [
            pltpu.VMEM((rows_y + 2, 3 * width_out, LANES), BF16),
            pltpu.VMEM((3 * width_in, 9 * width_out), BF16),
        ],
    )(side, gathered, taps)
    shares = lax.all_to_all(
        shares.reshape(n_co, rows_y // n_co, width_in, LANES), "co", 0, 0, tiled=True
    )
    input_grad = call(
        add_shares,
        shape((rows_y // n_co, width_in, LANES), F32),
        [VMEM],
        0,
        size * width_in,
    )(shares)
    weight_grad, bias_grad = call(
        finish_filter,
        (shape((27, width_out, width_in), F32), shape((1, width_out), F32)),
        [VMEM, VMEM],
        0,
        27 * 4 * width_in * width_out,
    )(packed, other)
    return (activated, input_grad, weight_grad.transpose(0, 2, 1), bias_grad.reshape(width_out))


def solution(mesh):
    placed = (P(None, "ci", "sp"), P(None, "ci", "co"), P("co"), P("ci", "co", "sp"))
    return jax.shard_map(
        local,
        mesh=mesh,
        in_specs=placed,
        out_specs=(P("ci", "co", "sp"), P("co", "ci", "sp"), P(None, "ci", "co"), P("co")),
        check_vma=False,
    )
```

```python
import jax
import jax.numpy as jnp
from jax import lax
from jax.experimental import pallas as pl
from jax.experimental.pallas import tpu as pltpu
from jax.sharding import PartitionSpec as P

SZ = 32
LANES = 128
BF16 = jnp.bfloat16
F32 = jnp.float32
VMEM = pl.BlockSpec(memory_space=pltpu.VMEM)
SMEM = pl.BlockSpec(memory_space=pltpu.SMEM)
HBM = pl.BlockSpec(memory_space=pltpu.HBM)
stay = pltpu.with_memory_space_constraint


def call(body, outs, specs, flops, moved, scratch=(), vmem=40):
    return pl.pallas_call(
        body,
        out_shape=outs,
        in_specs=specs,
        out_specs=jax.tree.map(lambda _: VMEM, outs),
        scratch_shapes=list(scratch),
        cost_estimate=pl.CostEstimate(flops=flops, bytes_accessed=moved, transcendentals=0),
        compiler_params=pltpu.CompilerParams(vmem_limit_bytes=vmem * 2**20),
    )


def lane(shape):
    return lax.broadcasted_iota(jnp.int32, shape, len(shape) - 1)


def pack_plane(side, planes):
    packed = None
    at = lane(planes[0].shape)
    for k, plane in enumerate(planes):
        moved = pltpu.roll(plane, lax.rem(SZ * k + SZ * (1 - side), LANES), 1)
        packed = moved if packed is None else jnp.where(at >= SZ * k, moved, packed)
    return packed


def neighbours(own, low=None, high=None, k=0):
    at = lane(own.shape)
    zero = jnp.zeros_like(own)
    left = zero if low is None else pltpu.roll(low, (-SZ * k) % LANES, 1)
    right = zero if high is None else pltpu.roll(high, (LANES - SZ - SZ * k) % LANES, 1)
    before = jnp.where(at < SZ, left, pltpu.roll(own, SZ, 1))
    after = jnp.where(at >= LANES - SZ, right, pltpu.roll(own, LANES - SZ, 1))
    return before, own, after


def split_halo(side, packed):
    zero = jnp.zeros_like(packed)
    return jnp.where(side == 1, packed, zero), jnp.where(side == 0, packed, zero)


def along_z(terms):
    lower, middle, upper = terms
    width = middle.shape[1]
    z = lane((middle.shape[0], LANES)) % SZ
    parts = []
    for start in range(0, width, LANES):
        cut = slice(start, start + LANES)
        parts.append(
            middle[:, cut]
            + jnp.where(z == 0, 0.0, pltpu.roll(lower[:, cut], 1, 1))
            + jnp.where(z == SZ - 1, 0.0, pltpu.roll(upper[:, cut], LANES - 1, 1))
        )
    return parts


def correlate_rows(taps, spread_ref, y, width):
    depth = 3 * spread_ref.shape[1]
    columns = jnp.concatenate(
        [spread_ref[pl.ds(y + k, 3)].reshape(depth, LANES) for k in range(2)], axis=1
    )
    product = jnp.dot(taps, columns, preferred_element_type=F32)
    parts = along_z([product[c * width : (c + 1) * width] for c in range(3)])
    return [part.astype(BF16) for part in parts]


def forward(
    side_ref, features_hbm, weight_hbm, out_ref,
    features_ref, weight_ref, spread_ref, taps_ref, edge_taps_ref, edge_ref, sems,
):
    rows_y, width_in, _ = features_ref.shape
    width_out = weight_ref.shape[1]
    groups = rows_y // 4
    pieces = sems.shape[0] - 1
    step = rows_y // pieces
    fetch = [
        pltpu.make_async_copy(
            features_hbm.at[pl.ds(k * step, step)], features_ref.at[pl.ds(k * step, step)], sems.at[k]
        )
        for k in range(pieces)
    ]
    fetch_weight = pltpu.make_async_copy(weight_hbm, weight_ref, sems.at[pieces])
    fetch[0].start()
    fetch_weight.start()
    for copy in fetch[1:]:
        copy.start()
    side = side_ref[0]
    blank = jnp.zeros(spread_ref.shape[1:], BF16)
    spread_ref[0] = blank
    spread_ref[rows_y + 1] = blank
    fetch_weight.wait()
    for c in range(3):
        rows = slice(c * width_out, (c + 1) * width_out)
        taps_ref[rows] = jnp.concatenate([weight_ref[3 * ab + c] for ab in range(9)], axis=1)
        edge_taps_ref[rows] = jnp.concatenate(
            [weight_ref[9 * a + c + 6 * side] for a in range(3)], axis=1
        )
    taps = taps_ref[...]

    done = 0
    for group in range(groups):
        if group * 4 % step == 0:
            fetch[group * 4 // step].wait()
        planes = [features_ref[4 * group + k] for k in range(4)]
        for k in range(4):
            seen = neighbours(planes[k])
            for b in range(3):
                spread_ref[4 * group + k + 1, b * width_in : (b + 1) * width_in] = seen[b]
        edge_ref[group + 1] = pack_plane(side, planes)
        while done + 2 < 4 * group + 4 or (group == groups - 1 and done < rows_y):
            parts = correlate_rows(taps, spread_ref, done, width_out)
            for k in range(2):
                start = (done + k) % 4 * width_out
                out_ref[done // 4, start : start + width_out] = parts[k]
            done += 2
    none = jnp.zeros(edge_ref.shape[1:], BF16)
    edge_ref[0] = none
    edge_ref[groups + 1] = none
    at = lane((width_in, LANES))
    columns = []
    for group in range(groups):
        last, here, following = (edge_ref[group + k] for k in range(3))
        above = jnp.where(at < SZ, pltpu.roll(last, SZ, 1), pltpu.roll(here, SZ, 1))
        below = jnp.where(
            at >= LANES - SZ,
            pltpu.roll(following, LANES - SZ, 1),
            pltpu.roll(here, LANES - SZ, 1),
        )
        columns.append(jnp.concatenate([above, here, below], axis=0))
    product = jnp.dot(
        edge_taps_ref[...], jnp.concatenate(columns, axis=1), preferred_element_type=F32
    )
    parts = along_z([product[c * width_out : (c + 1) * width_out] for c in range(3)])
    for group in range(groups):
        out_ref[group, 4 * width_out :] = parts[group].astype(BF16)


def reduce_rows(side_ref, shares_ref, cotangent_ref, own_ref, message_ref):
    total = shares_ref[0].astype(F32)
    for k in range(1, shares_ref.shape[0]):
        total = total + shares_ref[k].astype(F32)
    rows, width, _ = cotangent_ref.shape
    planes = [total[k * width : (k + 1) * width] for k in range(rows)]
    for k in range(rows):
        own_ref[k] = planes[k]
    side = side_ref[0]
    message_ref[0] = total[rows * width :]
    message_ref[1] = pack_plane(side, planes)
    message_ref[2] = pack_plane(side, [cotangent_ref[k].astype(F32) for k in range(rows)])


def bend(pre):
    return jnp.tanh(0.7978845608 * (pre + 0.044715 * (pre * pre * pre)))


def gelu_slope(pre, cotangent):
    bent = bend(pre)
    inner = 0.7978845608 * (1.0 + 3.0 * 0.044715 * (pre * pre))
    slope = 0.5 * (1.0 + bent) + 0.5 * pre * (1.0 - bent * bent) * inner
    return (cotangent * slope).astype(BF16)


def preactivation(side, own_ref, theirs_ref, bias):
    width = own_ref.shape[1]
    edge = lane((width, LANES)) // SZ == 3 * (1 - side)
    added = theirs_ref[0]
    rows = []
    for k in range(own_ref.shape[0]):
        moved = pltpu.roll(added, lax.rem(3 * SZ * (1 - side) - SZ * k + LANES, LANES), 1)
        rows.append(own_ref[k] + jnp.where(edge, moved, 0.0) + bias)
    return rows


def pointwise(side_ref, own_ref, mine_ref, theirs_ref, bias_ref, cotangent_ref, out_ref):
    bias = jnp.broadcast_to(bias_ref[...], own_ref.shape[1:])
    grads = [
        gelu_slope(pre, cotangent_ref[k].astype(F32))
        for k, pre in enumerate(preactivation(side_ref[0], own_ref, theirs_ref, bias))
    ]
    grads.append(gelu_slope(theirs_ref[1] + mine_ref[0] + bias, theirs_ref[2]))
    block = jnp.concatenate(grads, axis=0)
    for k in range(out_ref.shape[0]):
        out_ref[k] = block


def spread_gradient(side, gathered_ref, width, put):
    rows = 4 * width
    for group in range(gathered_ref.shape[0]):
        low, high = split_halo(side, gathered_ref[group, rows:])
        for k in range(4):
            own = gathered_ref[group, k * width : (k + 1) * width]
            put(4 * group + k, neighbours(own, low, high, k))


def backward(
    side_ref, core_ref, gathered_ref, weight_ref, mine_ref, other_ref, spread_ref, taps_ref
):
    slots, rows, width_in, _ = mine_ref.shape
    rows_y = 2 * slots * rows
    width_out = weight_ref.shape[1]
    core = core_ref[0]
    blank = jnp.zeros(spread_ref.shape[1:], BF16)
    spread_ref[0] = blank
    spread_ref[rows_y + 1] = blank

    def put(y, seen):
        for b in range(3):
            spread_ref[y + 1, b * width_out : (b + 1) * width_out] = seen[b]

    spread_gradient(side_ref[0], gathered_ref, width_out, put)
    for c in range(3):
        block = jnp.concatenate([weight_ref[26 - 3 * ab - c] for ab in range(9)], axis=0)
        taps_ref[c * width_in : (c + 1) * width_in] = block.T
    taps = taps_ref[...]
    for out_ref, owner in ((other_ref, 1 - core), (mine_ref, core)):
        for slot in range(slots):
            parts = correlate_rows(taps, spread_ref, 2 * rows * slot + rows * owner, width_in)
            for k in range(rows):
                out_ref[slot, k] = parts[k]


def add_pair(core_ref, mine_ref, others_ref, out_ref):
    other = others_ref[1 - core_ref[0]]
    out_ref[...] = (mine_ref[...].astype(F32) + other.astype(F32)).astype(BF16)


def filter_gradient(side_ref, features_ref, gathered_ref, out_ref, grad_ref, rows_ref):
    rows_y, width_in, _ = features_ref.shape
    width_out = grad_ref.shape[0] // 9
    z = lane((width_out, LANES)) % SZ
    zero = jnp.zeros((width_out, LANES), BF16)

    def put(y, seen):
        columns = slice(y * LANES, (y + 1) * LANES)
        for b in range(3):
            own = seen[2 - b]
            moved = (
                jnp.where(z == SZ - 1, zero, pltpu.roll(own, LANES - 1, 1)),
                own,
                jnp.where(z == 0, zero, pltpu.roll(own, 1, 1)),
            )
            for c in range(3):
                start = (3 * b + c) * width_out
                grad_ref[start : start + width_out, columns] = moved[c]

    spread_gradient(side_ref[0], gathered_ref, width_out, put)
    for a in range(3):
        for y in range(rows_y):
            source = y + a - 1
            inside = 0 <= source < rows_y
            rows_ref[a * width_in : (a + 1) * width_in, y * LANES : (y + 1) * LANES] = (
                features_ref[source] if inside else jnp.zeros((width_in, LANES), BF16)
            )
    over_voxels = (((1,), (1,)), ((), ()))
    grads = grad_ref[...]
    total = lax.dot_general(grads, rows_ref[...], over_voxels, preferred_element_type=F32)
    middle = 4 * width_out
    ones = jnp.ones((16, grads.shape[1]), BF16)
    bias = lax.dot_general(
        ones, grad_ref[middle : middle + width_out], over_voxels, preferred_element_type=F32
    )
    count = total.shape[0]
    rounded = total.astype(BF16)
    out_ref[:count] = rounded[:, : 2 * width_in]
    last = rounded[:, 2 * width_in :]
    out_ref[count : count + count // 2] = jnp.concatenate(
        [last[: count // 2], last[count // 2 :]], axis=1
    )
    high = bias.astype(BF16)
    rest = bias - high.astype(F32)
    mid = rest.astype(BF16)
    low = (rest - mid.astype(F32)).astype(BF16)
    row = lax.broadcasted_iota(jnp.int32, bias.shape, 0)
    nothing = jnp.zeros_like(bias)
    terms = jnp.where(
        row == 0,
        high.astype(F32),
        jnp.where(row == 1, mid.astype(F32), jnp.where(row == 2, low.astype(F32), nothing)),
    ).astype(BF16)
    out_ref[count + count // 2 :] = jnp.concatenate(
        [terms, jnp.zeros((16, LANES - width_out), BF16)], axis=1
    )


def finish(
    side_ref, shares_ref, own_ref, other_ref, sums_ref, theirs_ref, bias_vector_ref,
    input_ref, weight_ref, bias_ref, act_ref,
):
    total = shares_ref[0].astype(F32)
    for k in range(1, shares_ref.shape[0]):
        total = total + shares_ref[k].astype(F32)
    input_ref[...] = total
    bias = jnp.broadcast_to(bias_vector_ref[...], sums_ref.shape[1:])
    for k, pre in enumerate(preactivation(side_ref[0], sums_ref, theirs_ref, bias)):
        act_ref[k] = (0.5 * pre * (1.0 + bend(pre))).astype(BF16)
    _, width_out, width_in = weight_ref.shape
    count = 9 * width_out
    half = count // 2
    both = own_ref[...].astype(F32) + other_ref[...].astype(F32)
    for bc in range(9):
        rows = slice(bc * width_out, (bc + 1) * width_out)
        first = both[rows]
        weight_ref[bc] = first[:, :width_in]
        weight_ref[9 + bc] = first[:, width_in:]
        for step in range(0, width_out, 16):
            start = bc * width_out + step
            if start < half:
                piece = both[count + start : count + start + 16, :width_in]
            else:
                start -= half
                piece = both[count + start : count + start + 16, width_in:]
            weight_ref[18 + bc, step : step + 16] = piece
    first = count + half
    mine = own_ref[first:].astype(F32)
    theirs = other_ref[first:].astype(F32)
    bias_ref[...] = (
        jnp.sum(mine, axis=0, keepdims=True) + jnp.sum(theirs, axis=0, keepdims=True)
    )[:, :width_out]


def local(features, weight, bias_vector, cotangent):
    rows_y, width_in, _ = features.shape
    width_out = weight.shape[2]
    n_ci, n_co = lax.axis_size("ci"), lax.axis_size("co")
    shape = jax.ShapeDtypeStruct
    side = lax.axis_index("sp").astype(jnp.int32).reshape(1)
    core = lax.rem(lax.axis_index("co"), 2).astype(jnp.int32).reshape(1)
    side, core = lax.optimization_barrier((side, core))
    swap = [(0, 1), (1, 0)]
    taps = weight.transpose(0, 2, 1)
    work = 2 * 27 * rows_y * LANES * width_in * width_out
    size = rows_y * LANES * 2

    block = 5 * width_out
    partial = call(
        forward,
        pltpu.VMEM((n_ci, block, LANES), BF16),
        [SMEM, HBM, HBM],
        work,
        size * (width_in + width_out),
        [
            pltpu.VMEM(features.shape, BF16),
            pltpu.VMEM(taps.shape, BF16),
            pltpu.VMEM((rows_y + 2, 3 * width_in, LANES), BF16),
            pltpu.VMEM((3 * width_out, 9 * width_in), BF16),
            pltpu.VMEM((3 * width_out, 3 * width_in), BF16),
            pltpu.VMEM((rows_y // 4 + 2, width_in, LANES), BF16),
            pltpu.SemaphoreType.DMA((2,)),
        ],
    )(side, stay(features, pltpu.HBM), stay(taps, pltpu.HBM))
    shares = lax.all_to_all(partial, "ci", 0, 0, tiled=True)
    own, mine = call(
        reduce_rows,
        (shape(cotangent.shape, F32), shape((3, width_out, LANES), F32)),
        [SMEM, VMEM, VMEM],
        0,
        2 * size * width_out,
    )(side, shares, cotangent)
    theirs = lax.ppermute(mine, "sp", swap)
    bias_column = bias_vector.reshape(width_out, 1)
    copies = call(
        pointwise,
        pltpu.VMEM((n_ci, block, LANES), BF16),
        [SMEM, VMEM, VMEM, VMEM, VMEM, VMEM],
        0,
        2 * size * width_out,
    )(side, own, mine, theirs, bias_column, cotangent)
    gathered = lax.all_to_all(copies, "ci", 0, 0, tiled=True)
    packed = call(
        filter_gradient,
        shape((9 * width_out + 9 * width_out // 2 + 16, LANES), BF16),
        [SMEM, VMEM, VMEM],
        work,
        size * (width_in + width_out),
        [
            pltpu.VMEM((9 * width_out, rows_y * LANES), BF16),
            pltpu.VMEM((3 * width_in, rows_y * LANES), BF16),
        ],
    )(side, features, gathered)
    other = lax.ppermute(packed, "sp", swap)
    gathered, packed = lax.optimization_barrier((gathered, packed))
    quarter = (n_co // 2, rows_y // n_co, width_in, LANES)
    mine, other_half = call(
        backward,
        (pltpu.VMEM(quarter, BF16), pltpu.VMEM(quarter, BF16)),
        [SMEM, SMEM, VMEM, VMEM],
        work,
        size * (width_in + width_out),
        [
            pltpu.VMEM((rows_y + 2, 3 * width_out, LANES), BF16),
            pltpu.VMEM((3 * width_in, 9 * width_out), BF16),
        ],
    )(side, core, gathered, taps)
    pairs = [[k, k + 1] for k in range(0, n_co, 2)]
    halves = lax.all_gather(other_half, "co", axis=0, axis_index_groups=pairs)
    summed = call(
        add_pair, pltpu.VMEM(quarter, BF16), [SMEM, VMEM, VMEM], 0, size * width_in
    )(core, mine, halves)
    summed, other = lax.optimization_barrier((summed, other))
    same_core = [list(range(k, n_co, 2)) for k in range(2)]
    shares = lax.all_to_all(summed, "co", 0, 0, tiled=True, axis_index_groups=same_core)
    input_grad, weight_grad, bias_grad, activated = call(
        finish,
        (
            shape(quarter[1:], F32),
            shape((27, width_out, width_in), F32),
            shape((1, width_out), F32),
            shape(cotangent.shape, BF16),
        ),
        [SMEM] + [VMEM] * 6,
        0,
        27 * 4 * width_in * width_out,
    )(side, shares, packed, other, own, theirs, bias_column)
    return (activated, input_grad, weight_grad.transpose(0, 2, 1), bias_grad.reshape(width_out))


def solution(mesh):
    placed = (P(None, "ci", "sp"), P(None, "ci", "co"), P("co"), P("ci", "co", "sp"))
    return jax.shard_map(
        local,
        mesh=mesh,
        in_specs=placed,
        out_specs=(P("ci", "co", "sp"), P("co", "ci", "sp"), P(None, "ci", "co"), P("co")),
        check_vma=False,
    )
```

```python
import jax
import jax.numpy as jnp
from jax import lax
from jax.experimental import pallas as pl
from jax.experimental.pallas import tpu as pltpu
from jax.sharding import PartitionSpec as P

SZ = 32
LANES = 128
BF16 = jnp.bfloat16
F32 = jnp.float32
VMEM = pl.BlockSpec(memory_space=pltpu.VMEM)
SMEM = pl.BlockSpec(memory_space=pltpu.SMEM)
HBM = pl.BlockSpec(memory_space=pltpu.HBM)
stay = pltpu.with_memory_space_constraint


def call(body, outs, specs, flops, moved, scratch=(), vmem=40):
    return pl.pallas_call(
        body,
        out_shape=outs,
        in_specs=specs,
        out_specs=jax.tree.map(lambda _: VMEM, outs),
        scratch_shapes=list(scratch),
        cost_estimate=pl.CostEstimate(flops=flops, bytes_accessed=moved, transcendentals=0),
        compiler_params=pltpu.CompilerParams(vmem_limit_bytes=vmem * 2**20),
    )


def lane(shape):
    return lax.broadcasted_iota(jnp.int32, shape, len(shape) - 1)


def pack_plane(side, planes):
    packed = None
    at = lane(planes[0].shape)
    for k, plane in enumerate(planes):
        moved = pltpu.roll(plane, lax.rem(SZ * k + SZ * (1 - side), LANES), 1)
        packed = moved if packed is None else jnp.where(at >= SZ * k, moved, packed)
    return packed


def neighbours(own, left=None, right=None):
    at = lane(own.shape)
    zero = jnp.zeros_like(own)
    before = jnp.where(at < SZ, zero if left is None else left, pltpu.roll(own, SZ, 1))
    after = jnp.where(
        at >= LANES - SZ, zero if right is None else right, pltpu.roll(own, LANES - SZ, 1)
    )
    return before, own, after


def unpack_row(packed, row, target):
    half = LANES // 2
    return jnp.concatenate(
        [pltpu.roll(packed, (target - h * half - SZ * row) % LANES, 1) for h in range(2)], axis=0
    )


def pack_rows(rows, source):
    half = rows[0].shape[0] // 2
    at = lane((half, LANES))
    packed = None
    for k in range(4):
        h, row = divmod(k, 2)
        piece = rows[row][h * half : (h + 1) * half]
        moved = pltpu.roll(piece, (SZ * k - source) % LANES, 1)
        packed = moved if k == 0 else jnp.where(at >= SZ * k, moved, packed)
    return packed


def along_z(terms):
    lower, middle, upper = terms
    width = middle.shape[1]
    z = lane((middle.shape[0], LANES)) % SZ
    parts = []
    for start in range(0, width, LANES):
        cut = slice(start, start + LANES)
        parts.append(
            middle[:, cut]
            + jnp.where(z == 0, 0.0, pltpu.roll(lower[:, cut], 1, 1))
            + jnp.where(z == SZ - 1, 0.0, pltpu.roll(upper[:, cut], LANES - 1, 1))
        )
    return parts


def correlate_rows(taps, spread_ref, y, width):
    depth = 3 * spread_ref.shape[1]
    columns = jnp.concatenate(
        [spread_ref[pl.ds(y + k, 3)].reshape(depth, LANES) for k in range(2)], axis=1
    )
    product = jnp.dot(taps, columns, preferred_element_type=F32)
    parts = along_z([product[c * width : (c + 1) * width] for c in range(3)])
    return [part.astype(BF16) for part in parts]


def forward(
    side_ref, features_hbm, weight_hbm, bias_hbm, out_ref, column_ref,
    features_ref, weight_ref, bias_ref, spread_ref, taps_ref, edge_taps_ref, edge_ref, sems,
):
    rows_y, width_in, _ = features_ref.shape
    width_out = weight_ref.shape[1]
    groups = rows_y // 4
    fetch_weight = pltpu.make_async_copy(weight_hbm, weight_ref, sems.at[0])
    fetch = pltpu.make_async_copy(features_hbm, features_ref, sems.at[1])
    fetch_bias = pltpu.make_async_copy(bias_hbm, bias_ref, sems.at[2])
    fetch_weight.start()
    fetch.start()
    fetch_bias.start()
    side = side_ref[0]
    blank = jnp.zeros(spread_ref.shape[1:], BF16)
    spread_ref[0] = blank
    spread_ref[rows_y + 1] = blank
    fetch_weight.wait()
    for c in range(3):
        rows = slice(c * width_out, (c + 1) * width_out)
        taps_ref[rows] = jnp.concatenate([weight_ref[3 * ab + c] for ab in range(9)], axis=1)
        edge_taps_ref[rows] = jnp.concatenate(
            [weight_ref[9 * a + c + 6 * side] for a in range(3)], axis=1
        )
    taps = taps_ref[...]
    fetch_bias.wait()
    shape = (width_out, width_out)
    diagonal = lax.broadcasted_iota(jnp.int32, shape, 0) == lane(shape)
    column = jnp.sum(jnp.where(diagonal, bias_ref[...], 0.0), axis=1, keepdims=True)
    column_ref[...] = jnp.broadcast_to(column, column_ref.shape)
    fetch.wait()
    done = 0
    for group in range(groups):
        planes = [features_ref[4 * group + k] for k in range(4)]
        for k in range(4):
            seen = neighbours(planes[k])
            for b in range(3):
                spread_ref[4 * group + k + 1, b * width_in : (b + 1) * width_in] = seen[b]
        edge_ref[group + 1] = pack_plane(side, planes)
        while done + 2 < 4 * group + 4 or (group == groups - 1 and done < rows_y):
            parts = correlate_rows(taps, spread_ref, done, width_out)
            for k in range(2):
                out_ref[done // 2, k * width_out : (k + 1) * width_out] = parts[k]
            done += 2
    none = jnp.zeros(edge_ref.shape[1:], BF16)
    edge_ref[0] = none
    edge_ref[groups + 1] = none
    at = lane((width_in, LANES))
    columns = []
    for group in range(groups):
        last, here, following = (edge_ref[group + k] for k in range(3))
        above = jnp.where(at < SZ, pltpu.roll(last, SZ, 1), pltpu.roll(here, SZ, 1))
        below = jnp.where(
            at >= LANES - SZ,
            pltpu.roll(following, LANES - SZ, 1),
            pltpu.roll(here, LANES - SZ, 1),
        )
        columns.append(jnp.concatenate([above, here, below], axis=0))
    product = jnp.dot(
        edge_taps_ref[...], jnp.concatenate(columns, axis=1), preferred_element_type=F32
    )
    parts = along_z([product[c * width_out : (c + 1) * width_out] for c in range(3)])
    half = width_out // 2
    low = lane((half, LANES)) < LANES // 2
    for group in range(groups):
        here = parts[group]
        turned = pltpu.roll(here, LANES // 2, 1)
        first = jnp.where(low, here[:half], turned[half:])
        second = jnp.where(low, turned[:half], here[half:])
        out_ref[2 * group, 2 * width_out :] = first.astype(BF16)
        out_ref[2 * group + 1, 2 * width_out :] = second.astype(BF16)


def bend(pre):
    return jnp.tanh(0.7978845608 * (pre + 0.044715 * (pre * pre * pre)))


def gelu(pre, cotangent):
    bent = bend(pre)
    half = 0.5 * (1.0 + bent)
    inner = 0.7978845608 * (1.0 + 3.0 * 0.044715 * (pre * pre))
    slope = half + 0.5 * pre * (1.0 - bent * bent) * inner
    return (pre * half).astype(BF16), (cotangent.astype(F32) * slope).astype(BF16)


def pointwise(side_ref, shares_ref, bias_ref, own_ref, other_ref, act_ref, out_ref):
    width = own_ref.shape[1]
    lower, upper = side_ref[0] == 0, side_ref[0] == 1
    bias = bias_ref[...]
    sums = []
    for h in range(2):
        total = shares_ref[h].astype(F32)
        for k in range(2 + h, shares_ref.shape[0], 2):
            total = total + shares_ref[k].astype(F32)
        sums.append(total)
    at = lane((width, LANES))
    edges = (at >= LANES - SZ, at < SZ)
    grads = ([], [])
    for row in range(2):
        mine = own_ref[2 * side_ref[0] + row]
        theirs = other_ref[2 * side_ref[0] + row]
        cotangents = (jnp.where(lower, mine, theirs), jnp.where(upper, mine, theirs))
        acts = []
        for h in range(2):
            added = unpack_row(sums[1 - h][2 * width :], row, (LANES - SZ, 0)[h])
            pre = sums[h][row * width : (row + 1) * width]
            pre = pre + jnp.where(edges[h], added, 0.0) + bias
            act, grad = gelu(pre, cotangents[h])
            acts.append(act)
            grads[h].append(grad)
        act_ref[0, row] = jnp.where(lower, acts[0], acts[1])
        act_ref[1, row] = jnp.where(lower, acts[1], acts[0])
    blocks = [
        jnp.concatenate([*grads[h], pack_rows(grads[1 - h], (0, LANES - SZ)[h])], axis=0)
        for h in range(2)
    ]
    for k in range(out_ref.shape[0]):
        out_ref[k] = blocks[k % 2]


def spread_gradient(side, gathered_ref, width, put):
    for slot in range(gathered_ref.shape[0]):
        packed = gathered_ref[slot, 2 * width :]
        zero = jnp.zeros_like(packed)
        low = jnp.where(side == 1, packed, zero)
        high = jnp.where(side == 0, packed, zero)
        for row in range(2):
            own = gathered_ref[slot, row * width : (row + 1) * width]
            left = unpack_row(low, row, 0)
            right = unpack_row(high, row, LANES - SZ)
            put(2 * slot + row, neighbours(own, left, right))


def backward(
    side_ref, core_ref, gathered_ref, weight_ref, mine_ref, other_ref, spread_ref, taps_ref
):
    slots, rows, width_in, _ = mine_ref.shape
    rows_y = 2 * slots * rows
    width_out = weight_ref.shape[1]
    core = core_ref[0]
    blank = jnp.zeros(spread_ref.shape[1:], BF16)
    spread_ref[0] = blank
    spread_ref[rows_y + 1] = blank

    def put(y, seen):
        for b in range(3):
            spread_ref[y + 1, b * width_out : (b + 1) * width_out] = seen[b]

    spread_gradient(side_ref[0], gathered_ref, width_out, put)
    for c in range(3):
        block = jnp.concatenate([weight_ref[26 - 3 * ab - c] for ab in range(9)], axis=0)
        taps_ref[c * width_in : (c + 1) * width_in] = block.T
    taps = taps_ref[...]
    for out_ref, owner in ((other_ref, 1 - core), (mine_ref, core)):
        for slot in range(slots):
            parts = correlate_rows(taps, spread_ref, 2 * rows * slot + rows * owner, width_in)
            for k in range(rows):
                out_ref[slot, k] = parts[k]


def add_pair(mine_ref, other_ref, out_ref):
    out_ref[...] = (mine_ref[...].astype(F32) + other_ref[...].astype(F32)).astype(BF16)


def filter_gradient(
    side_ref, features_ref, gathered_ref, act_ref, out_ref, grad_ref, rows_ref
):
    rows_y, width_in, _ = features_ref.shape
    width_out = grad_ref.shape[0] // 9
    z = lane((width_out, LANES)) % SZ
    zero = jnp.zeros((width_out, LANES), BF16)

    def put(y, seen):
        columns = slice(y * LANES, (y + 1) * LANES)
        for b in range(3):
            own = seen[2 - b]
            moved = (
                jnp.where(z == SZ - 1, zero, pltpu.roll(own, LANES - 1, 1)),
                own,
                jnp.where(z == 0, zero, pltpu.roll(own, 1, 1)),
            )
            for c in range(3):
                start = (3 * b + c) * width_out
                grad_ref[start : start + width_out, columns] = moved[c]

    spread_gradient(side_ref[0], gathered_ref, width_out, put)
    for a in range(3):
        for y in range(rows_y):
            source = y + a - 1
            inside = 0 <= source < rows_y
            rows_ref[a * width_in : (a + 1) * width_in, y * LANES : (y + 1) * LANES] = (
                features_ref[source] if inside else jnp.zeros((width_in, LANES), BF16)
            )
    over_voxels = (((1,), (1,)), ((), ()))
    grads = grad_ref[...]
    total = lax.dot_general(grads, rows_ref[...], over_voxels, preferred_element_type=F32)
    middle = 4 * width_out
    ones = jnp.ones((16, grads.shape[1]), BF16)
    bias = lax.dot_general(
        ones, grad_ref[middle : middle + width_out], over_voxels, preferred_element_type=F32
    )
    count = total.shape[0]
    rounded = total
    out_ref[:count] = rounded[:, : 2 * width_in]
    last = rounded[:, 2 * width_in :]
    out_ref[count : count + count // 2] = jnp.concatenate(
        [last[: count // 2], last[count // 2 :]], axis=1
    )
    high = bias.astype(BF16)
    rest = bias - high.astype(F32)
    mid = rest.astype(BF16)
    low = (rest - mid.astype(F32)).astype(BF16)
    row = lax.broadcasted_iota(jnp.int32, bias.shape, 0)
    nothing = jnp.zeros_like(bias)
    terms = jnp.where(
        row == 0,
        high.astype(F32),
        jnp.where(row == 1, mid.astype(F32), jnp.where(row == 2, low.astype(F32), nothing)),
    ).astype(BF16)
    start = count + count // 2
    out_ref[start : start + 16] = jnp.concatenate(
        [terms.astype(F32), jnp.zeros((16, LANES - width_out), F32)], axis=1
    )
    out_ref[start + 16 :] = act_ref[1].reshape(2 * width_out, LANES).astype(F32)


def finish(
    side_ref, shares_ref, own_ref, other_ref, acted_ref, input_ref, weight_ref, bias_ref, act_ref
):
    total = shares_ref[0].astype(F32)
    for k in range(1, shares_ref.shape[0]):
        total = total + shares_ref[k].astype(F32)
    input_ref[...] = total
    side = side_ref[0]
    act_ref[pl.ds(2 * side, 2)] = acted_ref[0]
    received = other_ref[other_ref.shape[0] - 2 * acted_ref.shape[2] :]
    act_ref[pl.ds(2 - 2 * side, 2)] = received.reshape(acted_ref.shape[1:]).astype(BF16)
    _, width_out, width_in = weight_ref.shape
    count = 9 * width_out
    half = count // 2
    both = own_ref[...].astype(F32) + other_ref[...].astype(F32)
    for bc in range(9):
        rows = slice(bc * width_out, (bc + 1) * width_out)
        first = both[rows]
        weight_ref[bc] = first[:, :width_in]
        weight_ref[9 + bc] = first[:, width_in:]
        for step in range(0, width_out, 16):
            start = bc * width_out + step
            if start < half:
                piece = both[count + start : count + start + 16, :width_in]
            else:
                start -= half
                piece = both[count + start : count + start + 16, width_in:]
            weight_ref[18 + bc, step : step + 16] = piece
    first = count + half
    mine = own_ref[first : first + 16].astype(F32)
    theirs = other_ref[first : first + 16].astype(F32)
    bias_ref[...] = (
        jnp.sum(mine, axis=0, keepdims=True) + jnp.sum(theirs, axis=0, keepdims=True)
    )[:, :width_out]


def local(features, weight, bias_vector, cotangent):
    rows_y, width_in, _ = features.shape
    width_out = weight.shape[2]
    n_ci, n_co = lax.axis_size("ci"), lax.axis_size("co")
    shape = jax.ShapeDtypeStruct
    side = lax.axis_index("sp").astype(jnp.int32).reshape(1)
    core = lax.rem(lax.axis_index("co"), 2).astype(jnp.int32).reshape(1)
    side, core = lax.optimization_barrier((side, core))
    swap = [(0, 1), (1, 0)]
    taps = weight.transpose(0, 2, 1)
    work = 2 * 27 * rows_y * LANES * width_in * width_out
    size = rows_y * LANES * 2

    cotangent_other = lax.ppermute(cotangent, "sp", swap)
    block = (2 * n_ci, 2 * width_out + width_out // 2, LANES)
    partial, bias_columns = call(
        forward,
        (pltpu.VMEM(block, BF16), pltpu.VMEM((width_out, LANES), F32)),
        [SMEM, HBM, HBM, HBM],
        work,
        size * (width_in + width_out),
        [
            pltpu.VMEM(features.shape, BF16),
            pltpu.VMEM(taps.shape, BF16),
            pltpu.VMEM((1, width_out), F32),
            pltpu.VMEM((rows_y + 2, 3 * width_in, LANES), BF16),
            pltpu.VMEM((3 * width_out, 9 * width_in), BF16),
            pltpu.VMEM((3 * width_out, 3 * width_in), BF16),
            pltpu.VMEM((rows_y // 4 + 2, width_in, LANES), BF16),
            pltpu.SemaphoreType.DMA((3,)),
        ],
    )(side, *(stay(x, pltpu.HBM) for x in (features, taps, bias_vector.reshape(1, width_out))))
    both = ("ci", "sp")
    partial, cotangent_other = lax.optimization_barrier((partial, cotangent_other))
    shares = lax.all_to_all(partial, both, 0, 0, tiled=True)
    acted, copies = call(
        pointwise,
        (pltpu.VMEM((2, 2, width_out, LANES), BF16), pltpu.VMEM(block, BF16)),
        [SMEM, VMEM, VMEM, VMEM, VMEM],
        0,
        2 * size * width_out,
    )(side, shares, bias_columns, cotangent, cotangent_other)
    gathered = lax.all_to_all(copies, both, 0, 0, tiled=True)
    packed = call(
        filter_gradient,
        shape((9 * width_out + 9 * width_out // 2 + 16 + 2 * width_out, LANES), F32),
        [SMEM, VMEM, VMEM, VMEM],
        work,
        size * (width_in + width_out),
        [
            pltpu.VMEM((9 * width_out, rows_y * LANES), BF16),
            pltpu.VMEM((3 * width_in, rows_y * LANES), BF16),
        ],
    )(side, features, gathered, acted)
    quarter = (n_co // 2, rows_y // n_co, width_in, LANES)
    mine, other_half = call(
        backward,
        (pltpu.VMEM(quarter, BF16), pltpu.VMEM(quarter, BF16)),
        [SMEM, SMEM, VMEM, VMEM],
        work,
        size * (width_in + width_out),
        [
            pltpu.VMEM((rows_y + 2, 3 * width_out, LANES), BF16),
            pltpu.VMEM((3 * width_in, 9 * width_out), BF16),
        ],
    )(side, core, gathered, taps)
    received = lax.ppermute(other_half, "co", [(k, k ^ 1) for k in range(n_co)])
    received, packed = lax.optimization_barrier((received, packed))
    summed = call(
        add_pair, pltpu.VMEM(quarter, BF16), [VMEM, VMEM], 0, size * width_in
    )(mine, received)
    same_core = [list(range(k, n_co, 2)) for k in range(2)]
    shares = lax.all_to_all(summed, "co", 0, 0, tiled=True, axis_index_groups=same_core)
    other = lax.ppermute(packed, "sp", swap)
    input_grad, weight_grad, bias_grad, activated = call(
        finish,
        (
            shape(quarter[1:], F32),
            shape((27, width_out, width_in), F32),
            shape((1, width_out), F32),
            shape(cotangent.shape, BF16),
        ),
        [SMEM] + [VMEM] * 4,
        0,
        27 * 4 * width_in * width_out,
    )(side, shares, packed, other, acted)
    return (activated, input_grad, weight_grad.transpose(0, 2, 1), bias_grad.reshape(width_out))


def solution(mesh):
    placed = (P(None, "ci", "sp"), P(None, "ci", "co"), P("co"), P("ci", "co", "sp"))
    return jax.shard_map(
        local,
        mesh=mesh,
        in_specs=placed,
        out_specs=(P("ci", "co", "sp"), P("co", "ci", "sp"), P(None, "ci", "co"), P("co")),
        check_vma=False,
    )
```

```python
import jax
import jax.numpy as jnp
from jax import lax
from jax.experimental import pallas as pl
from jax.experimental.pallas import tpu as pltpu
from jax.sharding import PartitionSpec as P

SZ = 32
LANES = 128
BF16 = jnp.bfloat16
F32 = jnp.float32
VMEM = pl.BlockSpec(memory_space=pltpu.VMEM)
SMEM = pl.BlockSpec(memory_space=pltpu.SMEM)
HBM = pl.BlockSpec(memory_space=pltpu.HBM)
stay = pltpu.with_memory_space_constraint


def call(body, outs, specs, flops, moved, scratch=(), vmem=40):
    return pl.pallas_call(
        body,
        out_shape=outs,
        in_specs=specs,
        out_specs=jax.tree.map(lambda _: VMEM, outs),
        scratch_shapes=list(scratch),
        cost_estimate=pl.CostEstimate(flops=flops, bytes_accessed=moved, transcendentals=0),
        compiler_params=pltpu.CompilerParams(vmem_limit_bytes=vmem * 2**20),
    )


def lane(shape):
    return lax.broadcasted_iota(jnp.int32, shape, len(shape) - 1)


def pack_plane(side, planes):
    packed = None
    at = lane(planes[0].shape)
    for k, plane in enumerate(planes):
        moved = pltpu.roll(plane, lax.rem(SZ * k + SZ * (1 - side), LANES), 1)
        packed = moved if packed is None else jnp.where(at >= SZ * k, moved, packed)
    return packed


def neighbours(own):
    at = lane(own.shape)
    zero = jnp.zeros_like(own)
    before = jnp.where(at < SZ, zero, pltpu.roll(own, SZ, 1))
    after = jnp.where(at >= LANES - SZ, zero, pltpu.roll(own, LANES - SZ, 1))
    return before, own, after


def unpack_row(packed, row, target):
    half = LANES // 2
    return jnp.concatenate(
        [pltpu.roll(packed, (target - h * half - SZ * row) % LANES, 1) for h in range(2)], axis=0
    )


def pack_rows(rows, source):
    half = rows[0].shape[0] // 2
    at = lane((half, LANES))
    packed = None
    for k in range(4):
        h, row = divmod(k, 2)
        piece = rows[row][h * half : (h + 1) * half]
        moved = pltpu.roll(piece, lax.rem(SZ * k - source + LANES, LANES), 1)
        packed = moved if k == 0 else jnp.where(at >= SZ * k, moved, packed)
    return packed


def along_z(terms):
    lower, middle, upper = terms
    width = middle.shape[1]
    z = lane((middle.shape[0], LANES)) % SZ
    parts = []
    for start in range(0, width, LANES):
        cut = slice(start, start + LANES)
        parts.append(
            middle[:, cut]
            + jnp.where(z == 0, 0.0, pltpu.roll(lower[:, cut], 1, 1))
            + jnp.where(z == SZ - 1, 0.0, pltpu.roll(upper[:, cut], LANES - 1, 1))
        )
    return parts


def correlate_rows(taps, spread_ref, y, width):
    depth = 3 * spread_ref.shape[1]
    columns = jnp.concatenate(
        [spread_ref[pl.ds(y + k, 3)].reshape(depth, LANES) for k in range(2)], axis=1
    )
    product = jnp.dot(taps, columns, preferred_element_type=F32)
    parts = along_z([product[c * width : (c + 1) * width] for c in range(3)])
    return [part.astype(BF16) for part in parts]


def forward(
    side_ref, features_hbm, weight_hbm, bias_hbm, out_ref, column_ref,
    features_ref, weight_ref, bias_ref, spread_ref, taps_ref, edge_taps_ref, edge_ref, sems,
):
    rows_y, width_in, _ = features_ref.shape
    width_out = weight_ref.shape[1]
    groups = rows_y // 4
    fetch_weight = pltpu.make_async_copy(weight_hbm, weight_ref, sems.at[0])
    fetch = pltpu.make_async_copy(features_hbm, features_ref, sems.at[1])
    fetch_bias = pltpu.make_async_copy(bias_hbm, bias_ref, sems.at[2])
    fetch_weight.start()
    fetch.start()
    fetch_bias.start()
    side = side_ref[0]
    blank = jnp.zeros(spread_ref.shape[1:], BF16)
    spread_ref[0] = blank
    spread_ref[rows_y + 1] = blank
    fetch_weight.wait()
    for c in range(3):
        rows = slice(c * width_out, (c + 1) * width_out)
        taps_ref[rows] = jnp.concatenate([weight_ref[3 * ab + c] for ab in range(9)], axis=1)
        edge_taps_ref[rows] = jnp.concatenate(
            [weight_ref[9 * a + c + 6 * side] for a in range(3)], axis=1
        )
    taps = taps_ref[...]
    fetch_bias.wait()
    shape = (width_out, width_out)
    diagonal = lax.broadcasted_iota(jnp.int32, shape, 0) == lane(shape)
    column = jnp.sum(jnp.where(diagonal, bias_ref[...], 0.0), axis=1, keepdims=True)
    column_ref[...] = jnp.broadcast_to(column, column_ref.shape)
    fetch.wait()
    done = 0
    for group in range(groups):
        planes = [features_ref[4 * group + k] for k in range(4)]
        for k in range(4):
            seen = neighbours(planes[k])
            for b in range(3):
                spread_ref[4 * group + k + 1, b * width_in : (b + 1) * width_in] = seen[b]
        edge_ref[group + 1] = pack_plane(side, planes)
        while done + 2 < 4 * group + 4 or (group == groups - 1 and done < rows_y):
            parts = correlate_rows(taps, spread_ref, done, width_out)
            for k in range(2):
                out_ref[done // 2, k * width_out : (k + 1) * width_out] = parts[k]
            done += 2
    none = jnp.zeros(edge_ref.shape[1:], BF16)
    edge_ref[0] = none
    edge_ref[groups + 1] = none
    at = lane((width_in, LANES))
    columns = []
    for group in range(groups):
        last, here, following = (edge_ref[group + k] for k in range(3))
        above = jnp.where(at < SZ, pltpu.roll(last, SZ, 1), pltpu.roll(here, SZ, 1))
        below = jnp.where(
            at >= LANES - SZ,
            pltpu.roll(following, LANES - SZ, 1),
            pltpu.roll(here, LANES - SZ, 1),
        )
        columns.append(jnp.concatenate([above, here, below], axis=0))
    product = jnp.dot(
        edge_taps_ref[...], jnp.concatenate(columns, axis=1), preferred_element_type=F32
    )
    parts = along_z([product[c * width_out : (c + 1) * width_out] for c in range(3)])
    half = width_out // 2
    low = lane((half, LANES)) < LANES // 2
    for group in range(groups):
        here = parts[group]
        turned = pltpu.roll(here, LANES // 2, 1)
        first = jnp.where(low, here[:half], turned[half:])
        second = jnp.where(low, turned[:half], here[half:])
        out_ref[2 * group, 2 * width_out :] = first.astype(BF16)
        out_ref[2 * group + 1, 2 * width_out :] = second.astype(BF16)


def bend(pre):
    return jnp.tanh(0.7978845608 * (pre + 0.044715 * (pre * pre * pre)))


def gelu(pre, cotangent):
    bent = bend(pre)
    half = 0.5 * (1.0 + bent)
    inner = 0.7978845608 * (1.0 + 3.0 * 0.044715 * (pre * pre))
    slope = half + 0.5 * pre * (1.0 - bent * bent) * inner
    return (pre * half).astype(BF16), (cotangent.astype(F32) * slope).astype(BF16)


def pointwise(side_ref, shares_ref, bias_ref, own_ref, other_ref, act_ref, out_ref):
    width = own_ref.shape[1]
    lower, upper = side_ref[0] == 0, side_ref[0] == 1
    bias = bias_ref[...]
    sums = []
    for h in range(2):
        total = shares_ref[h].astype(F32)
        for k in range(2 + h, shares_ref.shape[0], 2):
            total = total + shares_ref[k].astype(F32)
        sums.append(total)
    at = lane((width, LANES))
    edges = (at >= LANES - SZ, at < SZ)
    grads = ([], [])
    for row in range(2):
        mine = own_ref[2 * side_ref[0] + row]
        theirs = other_ref[2 * side_ref[0] + row]
        cotangents = (jnp.where(lower, mine, theirs), jnp.where(upper, mine, theirs))
        acts = []
        for h in range(2):
            added = unpack_row(sums[1 - h][2 * width :], row, (LANES - SZ, 0)[h])
            pre = sums[h][row * width : (row + 1) * width]
            pre = pre + jnp.where(edges[h], added, 0.0) + bias
            act, grad = gelu(pre, cotangents[h])
            acts.append(act)
            grads[h].append(grad)
        act_ref[0, row] = jnp.where(lower, acts[0], acts[1])
        act_ref[1, row] = jnp.where(lower, acts[1], acts[0])
    blocks = [
        jnp.concatenate([*grads[h], pack_rows(grads[1 - h], (0, LANES - SZ)[h])], axis=0)
        for h in range(2)
    ]
    for k in range(out_ref.shape[0]):
        out_ref[k] = blocks[k % 2]


def backward(
    side_ref, core_ref, gathered_ref, weight_ref, mine_ref, other_ref, spread_ref, taps_ref,
):
    slots, rows, width_in, _ = mine_ref.shape
    rows_y = 2 * slots * rows
    width_out = weight_ref.shape[1]
    core = core_ref[0]
    blank = jnp.zeros(spread_ref.shape[1:], BF16)
    spread_ref[0] = blank
    spread_ref[rows_y + 1] = blank

    side = side_ref[0]
    half, at = width_out // 2, lane((width_out, LANES))
    target = (LANES - SZ) * (1 - side)
    for slot in range(gathered_ref.shape[0]):
        packed = gathered_ref[slot, 2 * width_out :]
        for row in range(2):
            beside = jnp.concatenate(
                [
                    pltpu.roll(packed, lax.rem(target + 2 * LANES - SZ * (2 * h + row), LANES), 1)
                    for h in range(2)
                ],
                axis=0,
            )
            zero = jnp.zeros_like(beside)
            own = gathered_ref[slot, row * width_out : (row + 1) * width_out]
            seen = (
                jnp.where(
                    at < SZ, jnp.where(side == 1, beside, zero), pltpu.roll(own, SZ, 1)
                ),
                own,
                jnp.where(
                    at >= LANES - SZ,
                    jnp.where(side == 0, beside, zero),
                    pltpu.roll(own, LANES - SZ, 1),
                ),
            )
            for b in range(3):
                spread_ref[2 * slot + row + 1, b * width_out : (b + 1) * width_out] = seen[b]
    for c in range(3):
        block = jnp.concatenate([weight_ref[26 - 3 * ab - c] for ab in range(9)], axis=0)
        taps_ref[c * width_in : (c + 1) * width_in] = block.T
    taps = taps_ref[...]
    for out_ref, owner in ((other_ref, 1 - core), (mine_ref, core)):
        for slot in range(slots):
            parts = correlate_rows(taps, spread_ref, 2 * rows * slot + rows * owner, width_in)
            for k in range(rows):
                out_ref[slot, k] = parts[k]


def add_pair(mine_ref, other_ref, out_ref):
    out_ref[...] = (mine_ref[...].astype(F32) + other_ref[...].astype(F32)).astype(BF16)


def filter_gradient(features_ref, spread_ref, act_ref, out_ref, grad_ref, rows_ref):
    rows_y, width_in, _ = features_ref.shape
    third = spread_ref.shape[1]
    width = third // 3
    z = lane((third, LANES)) % SZ
    zero = jnp.zeros((third, LANES), BF16)
    for y in range(rows_y):
        own = spread_ref[y + 1]
        moved = (
            jnp.where(z == SZ - 1, zero, pltpu.roll(own, LANES - 1, 1)),
            own,
            jnp.where(z == 0, zero, pltpu.roll(own, 1, 1)),
        )
        columns = slice(y * LANES, (y + 1) * LANES)
        for c in range(3):
            grad_ref[c * third : (c + 1) * third, columns] = moved[c]
        for a in range(3):
            source = y + a - 1
            inside = 0 <= source < rows_y
            rows_ref[a * width_in : (a + 1) * width_in, columns] = (
                features_ref[source] if inside else jnp.zeros((width_in, LANES), BF16)
            )
        rows_ref[3 * width_in :, columns] = jnp.ones((16, LANES), BF16)
    total = lax.dot_general(
        grad_ref[...], rows_ref[...], (((1,), (1,)), ((), ())), preferred_element_type=F32
    )
    count = total.shape[0]
    half = count // 2
    out_ref[:count] = total[:, : 2 * width_in]
    last = total[:, 2 * width_in : 3 * width_in]
    out_ref[count : count + half] = jnp.concatenate([last[:half], last[half:]], axis=1)
    start = count + half
    bias = total[third + width : third + 2 * width, 3 * width_in : 3 * width_in + 1]
    out_ref[start : start + width] = jnp.broadcast_to(bias, (width, LANES))
    out_ref[start + width :] = act_ref[1].reshape(2 * width, LANES).astype(F32)


def finish(
    side_ref, shares_ref, own_ref, other_ref, acted_ref, input_ref, weight_ref, bias_ref, act_ref
):
    total = shares_ref[0].astype(F32)
    for k in range(1, shares_ref.shape[0]):
        total = total + shares_ref[k].astype(F32)
    input_ref[...] = total
    side = side_ref[0]
    act_ref[pl.ds(2 * side, 2)] = acted_ref[0]
    received = other_ref[other_ref.shape[0] - 2 * acted_ref.shape[2] :]
    act_ref[pl.ds(2 - 2 * side, 2)] = received.reshape(acted_ref.shape[1:]).astype(BF16)
    _, width_out, width_in = weight_ref.shape
    count = 9 * width_out
    half = count // 2
    both = own_ref[: count + half + width_out] + other_ref[: count + half + width_out]
    for b in range(3):
        for c in range(3):
            start = (3 * c + 2 - b) * width_out
            first = both[start : start + width_out]
            weight_ref[3 * b + c] = first[:, :width_in]
            weight_ref[9 + 3 * b + c] = first[:, width_in:]
            for step in range(0, width_out, 16):
                row = start + step
                if row < half:
                    piece = both[count + row : count + row + 16, :width_in]
                else:
                    piece = both[half + row : half + row + 16, width_in:]
                weight_ref[18 + 3 * b + c, step : step + 16] = piece
    shape = (width_out, width_out)
    diagonal = lax.broadcasted_iota(jnp.int32, shape, 0) == lane(shape)
    sums = both[count + half :, :width_out]
    bias_ref[...] = jnp.sum(jnp.where(diagonal, sums, 0.0), axis=0, keepdims=True)


def local(features, weight, bias_vector, cotangent):
    rows_y, width_in, _ = features.shape
    width_out = weight.shape[2]
    n_ci, n_co = lax.axis_size("ci"), lax.axis_size("co")
    shape = jax.ShapeDtypeStruct
    side = lax.axis_index("sp").astype(jnp.int32).reshape(1)
    core = lax.rem(lax.axis_index("co"), 2).astype(jnp.int32).reshape(1)
    side, core = lax.optimization_barrier((side, core))
    swap = [(0, 1), (1, 0)]
    taps = weight.transpose(0, 2, 1)
    work = 2 * 27 * rows_y * LANES * width_in * width_out
    size = rows_y * LANES * 2

    cotangent_other = lax.ppermute(cotangent, "sp", swap)
    block = (2 * n_ci, 2 * width_out + width_out // 2, LANES)
    partial, bias_columns = call(
        forward,
        (pltpu.VMEM(block, BF16), pltpu.VMEM((width_out, LANES), F32)),
        [SMEM, HBM, HBM, HBM],
        work,
        size * (width_in + width_out),
        [
            pltpu.VMEM(features.shape, BF16),
            pltpu.VMEM(taps.shape, BF16),
            pltpu.VMEM((1, width_out), F32),
            pltpu.VMEM((rows_y + 2, 3 * width_in, LANES), BF16),
            pltpu.VMEM((3 * width_out, 9 * width_in), BF16),
            pltpu.VMEM((3 * width_out, 3 * width_in), BF16),
            pltpu.VMEM((rows_y // 4 + 2, width_in, LANES), BF16),
            pltpu.SemaphoreType.DMA((3,)),
        ],
    )(side, *(stay(x, pltpu.HBM) for x in (features, taps, bias_vector.reshape(1, width_out))))
    both = ("ci", "sp")
    partial, cotangent_other = lax.optimization_barrier((partial, cotangent_other))
    shares = lax.all_to_all(partial, both, 0, 0, tiled=True)
    acted, copies = call(
        pointwise,
        (pltpu.VMEM((2, 2, width_out, LANES), BF16), pltpu.VMEM(block, BF16)),
        [SMEM, VMEM, VMEM, VMEM, VMEM],
        0,
        2 * size * width_out,
    )(side, shares, bias_columns, cotangent, cotangent_other)
    gathered = lax.all_to_all(copies, both, 0, 0, tiled=True)
    quarter = (n_co // 2, rows_y // n_co, width_in, LANES)
    mine, other_half, spread = call(
        backward,
        (
            pltpu.VMEM(quarter, BF16),
            pltpu.VMEM(quarter, BF16),
            pltpu.VMEM((rows_y + 2, 3 * width_out, LANES), BF16),
        ),
        [SMEM, SMEM, VMEM, VMEM],
        work,
        size * (width_in + width_out),
        [pltpu.VMEM((3 * width_in, 9 * width_out), BF16)],
    )(side, core, gathered, taps)
    packed = call(
        filter_gradient,
        shape((9 * width_out + 9 * width_out // 2 + 3 * width_out, LANES), F32),
        [VMEM, VMEM, VMEM],
        work,
        size * (width_in + width_out),
        [
            pltpu.VMEM((9 * width_out, rows_y * LANES), BF16),
            pltpu.VMEM((3 * width_in + 16, rows_y * LANES), BF16),
        ],
    )(features, spread, acted)
    received = lax.ppermute(other_half, "co", [(k, k ^ 1) for k in range(n_co)])
    received, packed = lax.optimization_barrier((received, packed))
    summed = call(
        add_pair, pltpu.VMEM(quarter, BF16), [VMEM, VMEM], 0, size * width_in
    )(mine, received)
    same_core = [list(range(k, n_co, 2)) for k in range(2)]
    shares = lax.all_to_all(summed, "co", 0, 0, tiled=True, axis_index_groups=same_core)
    other = lax.ppermute(packed, "sp", swap)
    input_grad, weight_grad, bias_grad, activated = call(
        finish,
        (
            shape(quarter[1:], F32),
            shape((27, width_out, width_in), F32),
            shape((1, width_out), F32),
            shape(cotangent.shape, BF16),
        ),
        [SMEM] + [VMEM] * 4,
        0,
        27 * 4 * width_in * width_out,
    )(side, shares, packed, other, acted)
    return (activated, input_grad, weight_grad.transpose(0, 2, 1), bias_grad.reshape(width_out))


def solution(mesh):
    placed = (P(None, "ci", "sp"), P(None, "ci", "co"), P("co"), P("ci", "co", "sp"))
    return jax.shard_map(
        local,
        mesh=mesh,
        in_specs=placed,
        out_specs=(P("ci", "co", "sp"), P("co", "ci", "sp"), P(None, "ci", "co"), P("co")),
        check_vma=False,
    )
```

```python
import jax
import jax.numpy as jnp
from jax import lax
from jax.experimental import pallas as pl
from jax.experimental.pallas import tpu as pltpu
from jax.sharding import PartitionSpec as P

SZ = 32
LANES = 128
BF16 = jnp.bfloat16
F32 = jnp.float32
OVER_CI_SP = [0, 14, 12, 10, 8, 6, 4, 2, 1, 15, 13, 11, 9, 7, 5, 3]
OVER_CO = [0, 4, 1, 5, 2, 6, 3, 7]
VMEM = pl.BlockSpec(memory_space=pltpu.VMEM)
SMEM = pl.BlockSpec(memory_space=pltpu.SMEM)
HBM = pl.BlockSpec(memory_space=pltpu.HBM)
stay = pltpu.with_memory_space_constraint


def call(body, outs, specs, flops, moved, scratch=(), vmem=40):
    return pl.pallas_call(
        body,
        out_shape=outs,
        in_specs=specs,
        out_specs=jax.tree.map(lambda _: VMEM, outs),
        scratch_shapes=list(scratch),
        cost_estimate=pl.CostEstimate(flops=flops, bytes_accessed=moved, transcendentals=0),
        compiler_params=pltpu.CompilerParams(vmem_limit_bytes=vmem * 2**20),
    )


def lane(shape):
    return lax.broadcasted_iota(jnp.int32, shape, len(shape) - 1)


def pack_plane(side, planes):
    packed = None
    at = lane(planes[0].shape)
    for k, plane in enumerate(planes):
        moved = pltpu.roll(plane, lax.rem(SZ * k + SZ * (1 - side), LANES), 1)
        packed = moved if packed is None else jnp.where(at >= SZ * k, moved, packed)
    return packed


def neighbours(own):
    at = lane(own.shape)
    zero = jnp.zeros_like(own)
    before = jnp.where(at < SZ, zero, pltpu.roll(own, SZ, 1))
    after = jnp.where(at >= LANES - SZ, zero, pltpu.roll(own, LANES - SZ, 1))
    return before, own, after


def unpack_row(packed, row, target):
    half = LANES // 2
    return jnp.concatenate(
        [pltpu.roll(packed, (target - h * half - SZ * row) % LANES, 1) for h in range(2)], axis=0
    )


def pack_rows(rows, source):
    half = rows[0].shape[0] // 2
    at = lane((half, LANES))
    packed = None
    for k in range(4):
        h, row = divmod(k, 2)
        piece = rows[row][h * half : (h + 1) * half]
        moved = pltpu.roll(piece, lax.rem(SZ * k - source + LANES, LANES), 1)
        packed = moved if k == 0 else jnp.where(at >= SZ * k, moved, packed)
    return packed


def along_z(terms):
    lower, middle, upper = terms
    width = middle.shape[1]
    z = lane((middle.shape[0], LANES)) % SZ
    parts = []
    for start in range(0, width, LANES):
        cut = slice(start, start + LANES)
        parts.append(
            middle[:, cut]
            + jnp.where(z == 0, 0.0, pltpu.roll(lower[:, cut], 1, 1))
            + jnp.where(z == SZ - 1, 0.0, pltpu.roll(upper[:, cut], LANES - 1, 1))
        )
    return parts


def correlate_rows(taps, spread_ref, y, width):
    depth = 3 * spread_ref.shape[1]
    columns = jnp.concatenate(
        [spread_ref[y + k : y + k + 3].reshape(depth, LANES) for k in range(2)], axis=1
    )
    product = jnp.dot(taps, columns, preferred_element_type=F32)
    parts = along_z([product[c * width : (c + 1) * width] for c in range(3)])
    return [part.astype(BF16) for part in parts]


def forward(
    side_ref, features_hbm, weight_hbm, bias_hbm, out_ref, column_ref,
    features_ref, weight_ref, bias_ref, spread_ref, taps_ref, edge_taps_ref, edge_ref, sems,
):
    rows_y, width_in, _ = features_ref.shape
    width_out = weight_ref.shape[1]
    groups = rows_y // 4
    fetch_weight = pltpu.make_async_copy(weight_hbm, weight_ref, sems.at[0])
    fetch = pltpu.make_async_copy(features_hbm, features_ref, sems.at[1])
    fetch_bias = pltpu.make_async_copy(bias_hbm, bias_ref, sems.at[2])
    fetch_weight.start()
    fetch.start()
    fetch_bias.start()
    side = side_ref[0]
    blank = jnp.zeros(spread_ref.shape[1:], BF16)
    spread_ref[0] = blank
    spread_ref[rows_y + 1] = blank
    fetch_weight.wait()
    for c in range(3):
        rows = slice(c * width_out, (c + 1) * width_out)
        taps_ref[rows] = jnp.concatenate([weight_ref[3 * ab + c] for ab in range(9)], axis=1)
        edge_taps_ref[rows] = jnp.concatenate(
            [weight_ref[9 * a + c + 6 * side] for a in range(3)], axis=1
        )
    taps = taps_ref[...]
    fetch_bias.wait()
    shape = (width_out, width_out)
    diagonal = lax.broadcasted_iota(jnp.int32, shape, 0) == lane(shape)
    column = jnp.sum(jnp.where(diagonal, bias_ref[...], 0.0), axis=1, keepdims=True)
    column_ref[...] = jnp.broadcast_to(column, column_ref.shape)
    fetch.wait()
    done = 0
    for group in range(groups):
        planes = [features_ref[4 * group + k] for k in range(4)]
        for k in range(4):
            seen = neighbours(planes[k])
            for b in range(3):
                spread_ref[4 * group + k + 1, b * width_in : (b + 1) * width_in] = seen[b]
        edge_ref[group + 1] = pack_plane(side, planes)
        while done + 2 < 4 * group or (group == groups - 1 and done < rows_y):
            parts = correlate_rows(taps, spread_ref, done, width_out)
            for k in range(2):
                place = OVER_CI_SP.index(done // 2)
                out_ref[place, k * width_out : (k + 1) * width_out] = parts[k]
            done += 2
    none = jnp.zeros(edge_ref.shape[1:], BF16)
    edge_ref[0] = none
    edge_ref[groups + 1] = none
    at = lane((width_in, LANES))
    columns = []
    for group in range(groups):
        last, here, following = (edge_ref[group + k] for k in range(3))
        above = jnp.where(at < SZ, pltpu.roll(last, SZ, 1), pltpu.roll(here, SZ, 1))
        below = jnp.where(
            at >= LANES - SZ,
            pltpu.roll(following, LANES - SZ, 1),
            pltpu.roll(here, LANES - SZ, 1),
        )
        columns.append(jnp.concatenate([above, here, below], axis=0))
    product = jnp.dot(
        edge_taps_ref[...], jnp.concatenate(columns, axis=1), preferred_element_type=F32
    )
    parts = along_z([product[c * width_out : (c + 1) * width_out] for c in range(3)])
    half = width_out // 2
    low = lane((half, LANES)) < LANES // 2
    for group in range(groups):
        here = parts[group]
        turned = pltpu.roll(here, LANES // 2, 1)
        first = jnp.where(low, here[:half], turned[half:])
        second = jnp.where(low, turned[:half], here[half:])
        for k, part in enumerate((first, second)):
            place = OVER_CI_SP.index(2 * group + k)
            out_ref[place, 2 * width_out :] = part.astype(BF16)


def bend(pre):
    return jnp.tanh(0.7978845608 * (pre + 0.044715 * (pre * pre * pre)))


def gelu(pre, cotangent):
    bent = bend(pre)
    half = 0.5 * (1.0 + bent)
    inner = 0.7978845608 * (1.0 + 3.0 * 0.044715 * (pre * pre))
    slope = half + 0.5 * pre * (1.0 - bent * bent) * inner
    return (pre * half).astype(BF16), (cotangent.astype(F32) * slope).astype(BF16)


def pointwise(side_ref, shares_ref, bias_ref, own_ref, other_ref, act_ref, out_ref):
    width = own_ref.shape[1]
    lower, upper = side_ref[0] == 0, side_ref[0] == 1
    bias = bias_ref[...]
    sums = []
    for h in range(2):
        places = [k for k, owner in enumerate(OVER_CI_SP) if owner % 2 == h]
        total = shares_ref[places[0]].astype(F32)
        for k in places[1:]:
            total = total + shares_ref[k].astype(F32)
        sums.append(total)
    at = lane((width, LANES))
    edges = (at >= LANES - SZ, at < SZ)
    grads = ([], [])
    for row in range(2):
        mine = own_ref[2 * side_ref[0] + row]
        theirs = other_ref[2 * side_ref[0] + row]
        cotangents = (jnp.where(lower, mine, theirs), jnp.where(upper, mine, theirs))
        acts = []
        for h in range(2):
            added = unpack_row(sums[1 - h][2 * width :], row, (LANES - SZ, 0)[h])
            pre = sums[h][row * width : (row + 1) * width]
            pre = pre + jnp.where(edges[h], added, 0.0) + bias
            act, grad = gelu(pre, cotangents[h])
            acts.append(act)
            grads[h].append(grad)
        act_ref[0, row] = jnp.where(lower, acts[0], acts[1])
        act_ref[1, row] = jnp.where(lower, acts[1], acts[0])
    blocks = [
        jnp.concatenate([*grads[h], pack_rows(grads[1 - h], (0, LANES - SZ)[h])], axis=0)
        for h in range(2)
    ]
    for k in range(out_ref.shape[0]):
        out_ref[k] = blocks[OVER_CI_SP[k] % 2]


def backward(
    side_ref, core_ref, gathered_ref, weight_ref, mine_ref, other_ref, spread_ref, taps_ref,
):
    slots, rows, width_in, _ = mine_ref.shape
    rows_y = 2 * slots * rows
    width_out = weight_ref.shape[1]
    core = core_ref[0]
    blank = jnp.zeros(spread_ref.shape[1:], BF16)
    spread_ref[0] = blank
    spread_ref[rows_y + 1] = blank

    for c in range(3):
        block = jnp.concatenate([weight_ref[26 - 3 * ab - c] for ab in range(9)], axis=0)
        taps_ref[c * width_in : (c + 1) * width_in] = block.T
    taps = taps_ref[...]
    side = side_ref[0]
    half, at = width_out // 2, lane((width_out, LANES))
    target = (LANES - SZ) * (1 - side)
    done = 0
    for slot in range(2 * slots):
        place = OVER_CI_SP.index(slot)
        packed = gathered_ref[place, 2 * width_out :]
        for row in range(2):
            beside = jnp.concatenate(
                [
                    pltpu.roll(packed, lax.rem(target + 2 * LANES - SZ * (2 * h + row), LANES), 1)
                    for h in range(2)
                ],
                axis=0,
            )
            zero = jnp.zeros_like(beside)
            own = gathered_ref[place, row * width_out : (row + 1) * width_out]
            seen = (
                jnp.where(
                    at < SZ, jnp.where(side == 1, beside, zero), pltpu.roll(own, SZ, 1)
                ),
                own,
                jnp.where(
                    at >= LANES - SZ,
                    jnp.where(side == 0, beside, zero),
                    pltpu.roll(own, LANES - SZ, 1),
                ),
            )
            for b in range(3):
                spread_ref[2 * slot + row + 1, b * width_out : (b + 1) * width_out] = seen[b]
        while 4 * done + 4 < 2 * slot + 2 or (slot == 2 * slots - 1 and done < slots):
            pairs = [correlate_rows(taps, spread_ref, 4 * done + 2 * k, width_in) for k in range(2)]
            for k in range(rows):
                owner = OVER_CO.index(done)
                mine_ref[owner, k] = jnp.where(core == 0, pairs[0][k], pairs[1][k])
                other_ref[owner, k] = jnp.where(core == 0, pairs[1][k], pairs[0][k])
            done += 1


def add_pair(mine_ref, other_ref, out_ref):
    out_ref[...] = (mine_ref[...].astype(F32) + other_ref[...].astype(F32)).astype(BF16)


def filter_gradient(features_ref, spread_ref, act_ref, out_ref, grad_ref, rows_ref):
    rows_y, width_in, _ = features_ref.shape
    third = spread_ref.shape[1]
    width = third // 3
    z = lane((third, LANES)) % SZ
    zero = jnp.zeros((third, LANES), BF16)
    for y in range(rows_y):
        own = spread_ref[y + 1]
        moved = (
            jnp.where(z == SZ - 1, zero, pltpu.roll(own, LANES - 1, 1)),
            own,
            jnp.where(z == 0, zero, pltpu.roll(own, 1, 1)),
        )
        columns = slice(y * LANES, (y + 1) * LANES)
        for c in range(3):
            grad_ref[c * third : (c + 1) * third, columns] = moved[c]
        for a in range(3):
            source = y + a - 1
            inside = 0 <= source < rows_y
            rows_ref[a * width_in : (a + 1) * width_in, columns] = (
                features_ref[source] if inside else jnp.zeros((width_in, LANES), BF16)
            )
        rows_ref[3 * width_in :, columns] = jnp.ones((16, LANES), BF16)
    total = lax.dot_general(
        grad_ref[...], rows_ref[...], (((1,), (1,)), ((), ())), preferred_element_type=F32
    )
    count = total.shape[0]
    half = count // 2
    out_ref[:count] = total[:, : 2 * width_in]
    last = total[:, 2 * width_in : 3 * width_in]
    out_ref[count : count + half] = jnp.concatenate([last[:half], last[half:]], axis=1)
    start = count + half
    bias = total[third + width : third + 2 * width, 3 * width_in : 3 * width_in + 1]
    out_ref[start : start + width] = jnp.broadcast_to(bias, (width, LANES))
    out_ref[start + width :] = act_ref[1].reshape(2 * width, LANES).astype(F32)


def finish(
    side_ref, shares_ref, own_ref, other_ref, acted_ref, input_ref, weight_ref, bias_ref, act_ref
):
    total = shares_ref[0].astype(F32)
    for k in range(1, shares_ref.shape[0]):
        total = total + shares_ref[k].astype(F32)
    input_ref[...] = total
    side = side_ref[0]
    act_ref[pl.ds(2 * side, 2)] = acted_ref[0]
    received = other_ref[other_ref.shape[0] - 2 * acted_ref.shape[2] :]
    act_ref[pl.ds(2 - 2 * side, 2)] = received.reshape(acted_ref.shape[1:]).astype(BF16)
    _, width_out, width_in = weight_ref.shape
    count = 9 * width_out
    half = count // 2
    both = own_ref[: count + half + width_out] + other_ref[: count + half + width_out]
    for b in range(3):
        for c in range(3):
            start = (3 * c + 2 - b) * width_out
            first = both[start : start + width_out]
            weight_ref[3 * b + c] = first[:, :width_in]
            weight_ref[9 + 3 * b + c] = first[:, width_in:]
            for step in range(0, width_out, 16):
                row = start + step
                if row < half:
                    piece = both[count + row : count + row + 16, :width_in]
                else:
                    piece = both[half + row : half + row + 16, width_in:]
                weight_ref[18 + 3 * b + c, step : step + 16] = piece
    shape = (width_out, width_out)
    diagonal = lax.broadcasted_iota(jnp.int32, shape, 0) == lane(shape)
    sums = both[count + half :, :width_out]
    bias_ref[...] = jnp.sum(jnp.where(diagonal, sums, 0.0), axis=0, keepdims=True)


def local(features, weight, bias_vector, cotangent):
    rows_y, width_in, _ = features.shape
    width_out = weight.shape[2]
    n_ci, n_co = lax.axis_size("ci"), lax.axis_size("co")
    shape = jax.ShapeDtypeStruct
    side = lax.axis_index("sp").astype(jnp.int32).reshape(1)
    core = lax.rem(lax.axis_index("co"), 2).astype(jnp.int32).reshape(1)
    side, core = lax.optimization_barrier((side, core))
    swap = [(0, 1), (1, 0)]
    taps = weight.transpose(0, 2, 1)
    work = 2 * 27 * rows_y * LANES * width_in * width_out
    size = rows_y * LANES * 2

    cotangent_other = lax.ppermute(cotangent, "sp", swap)
    block = (2 * n_ci, 2 * width_out + width_out // 2, LANES)
    partial, bias_columns = call(
        forward,
        (pltpu.VMEM(block, BF16), pltpu.VMEM((width_out, LANES), F32)),
        [SMEM, HBM, HBM, HBM],
        work,
        size * (width_in + width_out),
        [
            pltpu.VMEM(features.shape, BF16),
            pltpu.VMEM(taps.shape, BF16),
            pltpu.VMEM((1, width_out), F32),
            pltpu.VMEM((rows_y + 2, 3 * width_in, LANES), BF16),
            pltpu.VMEM((3 * width_out, 9 * width_in), BF16),
            pltpu.VMEM((3 * width_out, 3 * width_in), BF16),
            pltpu.VMEM((rows_y // 4 + 2, width_in, LANES), BF16),
            pltpu.SemaphoreType.DMA((3,)),
        ],
    )(side, *(stay(x, pltpu.HBM) for x in (features, taps, bias_vector.reshape(1, width_out))))
    both = ("ci", "sp")
    partial, cotangent_other = lax.optimization_barrier((partial, cotangent_other))
    shares = lax.all_to_all(partial, both, 0, 0, tiled=True, axis_index_groups=[OVER_CI_SP])
    acted, copies = call(
        pointwise,
        (pltpu.VMEM((2, 2, width_out, LANES), BF16), pltpu.VMEM(block, BF16)),
        [SMEM, VMEM, VMEM, VMEM, VMEM],
        0,
        2 * size * width_out,
    )(side, shares, bias_columns, cotangent, cotangent_other)
    gathered = lax.all_to_all(copies, both, 0, 0, tiled=True, axis_index_groups=[OVER_CI_SP])
    quarter = (n_co // 2, rows_y // n_co, width_in, LANES)
    mine, other_half, spread = call(
        backward,
        (
            pltpu.VMEM(quarter, BF16),
            pltpu.VMEM(quarter, BF16),
            pltpu.VMEM((rows_y + 2, 3 * width_out, LANES), BF16),
        ),
        [SMEM, SMEM, VMEM, VMEM],
        work,
        size * (width_in + width_out),
        [pltpu.VMEM((3 * width_in, 9 * width_out), BF16)],
    )(side, core, gathered, taps)
    packed = call(
        filter_gradient,
        shape((9 * width_out + 9 * width_out // 2 + 3 * width_out, LANES), F32),
        [VMEM, VMEM, VMEM],
        work,
        size * (width_in + width_out),
        [
            pltpu.VMEM((9 * width_out, rows_y * LANES), BF16),
            pltpu.VMEM((3 * width_in + 16, rows_y * LANES), BF16),
        ],
    )(features, spread, acted)
    received = lax.ppermute(other_half, "co", [(k, k ^ 1) for k in range(n_co)])
    received, packed = lax.optimization_barrier((received, packed))
    summed = call(
        add_pair, pltpu.VMEM(quarter, BF16), [VMEM, VMEM], 0, size * width_in
    )(mine, received)
    same_core = [[2 * k + core_at for k in OVER_CO] for core_at in range(2)]
    shares = lax.all_to_all(summed, "co", 0, 0, tiled=True, axis_index_groups=same_core)
    other = lax.ppermute(packed, "sp", swap)
    input_grad, weight_grad, bias_grad, activated = call(
        finish,
        (
            shape(quarter[1:], F32),
            shape((27, width_out, width_in), F32),
            shape((1, width_out), F32),
            shape(cotangent.shape, BF16),
        ),
        [SMEM] + [VMEM] * 4,
        0,
        27 * 4 * width_in * width_out,
    )(side, shares, packed, other, acted)
    return (activated, input_grad, weight_grad.transpose(0, 2, 1), bias_grad.reshape(width_out))


def solution(mesh):
    placed = (P(None, "ci", "sp"), P(None, "ci", "co"), P("co"), P("ci", "co", "sp"))
    return jax.shard_map(
        local,
        mesh=mesh,
        in_specs=placed,
        out_specs=(P("ci", "co", "sp"), P("co", "ci", "sp"), P(None, "ci", "co"), P("co")),
        check_vma=False,
    )
```

```python
import jax
import jax.numpy as jnp
from jax import lax
from jax.experimental import pallas as pl
from jax.experimental.pallas import tpu as pltpu
from jax.sharding import PartitionSpec as P

SZ = 32
LANES = 128
BF16 = jnp.bfloat16
F32 = jnp.float32
OVER_CI_SP = [0, 14, 12, 10, 8, 6, 4, 2, 1, 15, 13, 11, 9, 7, 5, 3]
OVER_CO = [0, 4, 1, 5, 2, 6, 3, 7]
VMEM = pl.BlockSpec(memory_space=pltpu.VMEM)
SMEM = pl.BlockSpec(memory_space=pltpu.SMEM)
HBM = pl.BlockSpec(memory_space=pltpu.HBM)
stay = pltpu.with_memory_space_constraint


def call(body, outs, specs, flops, moved, scratch=(), vmem=40):
    return pl.pallas_call(
        body,
        out_shape=outs,
        in_specs=specs,
        out_specs=jax.tree.map(lambda _: VMEM, outs),
        scratch_shapes=list(scratch),
        cost_estimate=pl.CostEstimate(flops=flops, bytes_accessed=moved, transcendentals=0),
        compiler_params=pltpu.CompilerParams(vmem_limit_bytes=vmem * 2**20),
    )


def lane(shape):
    return lax.broadcasted_iota(jnp.int32, shape, len(shape) - 1)


def pack_plane(side, planes):
    packed = None
    at = lane(planes[0].shape)
    for k, plane in enumerate(planes):
        moved = pltpu.roll(plane, lax.rem(SZ * k + SZ * (1 - side), LANES), 1)
        packed = moved if packed is None else jnp.where(at >= SZ * k, moved, packed)
    return packed


def neighbours(own):
    at = lane(own.shape)
    zero = jnp.zeros_like(own)
    before = jnp.where(at < SZ, zero, pltpu.roll(own, SZ, 1))
    after = jnp.where(at >= LANES - SZ, zero, pltpu.roll(own, LANES - SZ, 1))
    return before, own, after


def unpack_row(packed, row, target):
    half = LANES // 2
    return jnp.concatenate(
        [pltpu.roll(packed, (target - h * half - SZ * row) % LANES, 1) for h in range(2)], axis=0
    )


def pack_rows(rows, source):
    half = rows[0].shape[0] // 2
    at = lane((half, LANES))
    packed = None
    for k in range(4):
        h, row = divmod(k, 2)
        piece = rows[row][h * half : (h + 1) * half]
        moved = pltpu.roll(piece, lax.rem(SZ * k - source + LANES, LANES), 1)
        packed = moved if k == 0 else jnp.where(at >= SZ * k, moved, packed)
    return packed


def along_z(terms):
    lower, middle, upper = terms
    width = middle.shape[1]
    z = lane((middle.shape[0], LANES)) % SZ
    parts = []
    for start in range(0, width, LANES):
        cut = slice(start, start + LANES)
        parts.append(
            middle[:, cut]
            + jnp.where(z == 0, 0.0, pltpu.roll(lower[:, cut], 1, 1))
            + jnp.where(z == SZ - 1, 0.0, pltpu.roll(upper[:, cut], LANES - 1, 1))
        )
    return parts


def correlate_rows(taps, spread_ref, y, width, own_ref=None):
    def row(at):
        rows = spread_ref[at]
        if own_ref is None:
            return [rows]
        inside = 1 <= at <= own_ref.shape[0]
        own = own_ref[at - 1] if inside else jnp.zeros(own_ref.shape[1:], BF16)
        return [rows[: own.shape[0]], own, rows[own.shape[0] :]]

    columns = jnp.concatenate(
        [jnp.concatenate(sum((row(y + k + a) for a in range(3)), []), axis=0) for k in range(2)],
        axis=1,
    )
    product = jnp.dot(taps, columns, preferred_element_type=F32)
    parts = along_z([product[c * width : (c + 1) * width] for c in range(3)])
    return [part.astype(BF16) for part in parts]


def forward(
    side_ref, features_hbm, weight_hbm, bias_hbm, out_ref, column_ref,
    features_ref, weight_ref, bias_ref, spread_ref, taps_ref, edge_taps_ref, edge_ref, sems,
):
    rows_y, width_in, _ = features_ref.shape
    width_out = weight_ref.shape[1]
    groups = rows_y // 4
    fetch_weight = pltpu.make_async_copy(weight_hbm, weight_ref, sems.at[0])
    step = rows_y // 2
    fetch = [
        pltpu.make_async_copy(
            features_hbm.at[pl.ds(k * step, step)],
            features_ref.at[pl.ds(k * step, step)],
            sems.at[2 + k],
        )
        for k in range(2)
    ]
    fetch_bias = pltpu.make_async_copy(bias_hbm, bias_ref, sems.at[1])
    fetch_weight.start()
    for copy in fetch:
        copy.start()
    fetch_bias.start()
    side = side_ref[0]
    blank = jnp.zeros(spread_ref.shape[1:], BF16)
    spread_ref[0] = blank
    spread_ref[rows_y + 1] = blank
    fetch_weight.wait()
    for c in range(3):
        rows = slice(c * width_out, (c + 1) * width_out)
        taps_ref[rows] = jnp.concatenate([weight_ref[3 * ab + c] for ab in range(9)], axis=1)
        edge_taps_ref[rows] = jnp.concatenate(
            [weight_ref[9 * a + c + 6 * side] for a in range(3)], axis=1
        )
    taps = taps_ref[...]
    fetch_bias.wait()
    shape = (width_out, width_out)
    diagonal = lax.broadcasted_iota(jnp.int32, shape, 0) == lane(shape)
    column = jnp.sum(jnp.where(diagonal, bias_ref[...], 0.0), axis=1, keepdims=True)
    column_ref[...] = jnp.broadcast_to(column, column_ref.shape)
    for copy in fetch:
        copy.wait()
    done = 0
    for group in range(groups):
        planes = [features_ref[4 * group + k] for k in range(4)]
        for k in range(4):
            seen = neighbours(planes[k])
            for b in (0, 2):
                spread_ref[4 * group + k + 1, b // 2 * width_in : (b // 2 + 1) * width_in] = seen[b]
        edge_ref[group + 1] = pack_plane(side, planes)
        while done + 2 < 4 * group or (group == groups - 1 and done < rows_y):
            parts = correlate_rows(taps, spread_ref, done, width_out, features_ref)
            for k in range(2):
                place = OVER_CI_SP.index(done // 2)
                out_ref[place, k * width_out : (k + 1) * width_out] = parts[k]
            done += 2
    none = jnp.zeros(edge_ref.shape[1:], BF16)
    edge_ref[0] = none
    edge_ref[groups + 1] = none
    at = lane((width_in, LANES))
    columns = []
    for group in range(groups):
        last, here, following = (edge_ref[group + k] for k in range(3))
        above = jnp.where(at < SZ, pltpu.roll(last, SZ, 1), pltpu.roll(here, SZ, 1))
        below = jnp.where(
            at >= LANES - SZ,
            pltpu.roll(following, LANES - SZ, 1),
            pltpu.roll(here, LANES - SZ, 1),
        )
        columns.append(jnp.concatenate([above, here, below], axis=0))
    product = jnp.dot(
        edge_taps_ref[...], jnp.concatenate(columns, axis=1), preferred_element_type=F32
    )
    parts = along_z([product[c * width_out : (c + 1) * width_out] for c in range(3)])
    half = width_out // 2
    low = lane((half, LANES)) < LANES // 2
    for group in range(groups):
        here = parts[group]
        turned = pltpu.roll(here, LANES // 2, 1)
        first = jnp.where(low, here[:half], turned[half:])
        second = jnp.where(low, turned[:half], here[half:])
        for k, part in enumerate((first, second)):
            place = OVER_CI_SP.index(2 * group + k)
            out_ref[place, 2 * width_out :] = part.astype(BF16)


def bend(pre):
    return jnp.tanh(0.7978845608 * (pre + 0.044715 * (pre * pre * pre)))


def gelu(pre, cotangent):
    bent = bend(pre)
    half = 0.5 * (1.0 + bent)
    inner = 0.7978845608 * (1.0 + 3.0 * 0.044715 * (pre * pre))
    slope = half + 0.5 * pre * (1.0 - bent * bent) * inner
    return (pre * half).astype(BF16), (cotangent.astype(F32) * slope).astype(BF16)


def pointwise(side_ref, shares_ref, bias_ref, own_ref, other_ref, act_ref, out_ref):
    width = own_ref.shape[1]
    lower, upper = side_ref[0] == 0, side_ref[0] == 1
    bias = bias_ref[...]
    sums = []
    for h in range(2):
        places = [k for k, owner in enumerate(OVER_CI_SP) if owner % 2 == h]
        total = shares_ref[places[0]].astype(F32)
        for k in places[1:]:
            total = total + shares_ref[k].astype(F32)
        sums.append(total)
    at = lane((width, LANES))
    edges = (at >= LANES - SZ, at < SZ)
    grads = ([], [])
    for row in range(2):
        mine = own_ref[2 * side_ref[0] + row]
        theirs = other_ref[2 * side_ref[0] + row]
        cotangents = (jnp.where(lower, mine, theirs), jnp.where(upper, mine, theirs))
        acts = []
        for h in range(2):
            added = unpack_row(sums[1 - h][2 * width :], row, (LANES - SZ, 0)[h])
            pre = sums[h][row * width : (row + 1) * width]
            pre = pre + jnp.where(edges[h], added, 0.0) + bias
            act, grad = gelu(pre, cotangents[h])
            acts.append(act)
            grads[h].append(grad)
        act_ref[0, row] = jnp.where(lower, acts[0], acts[1])
        act_ref[1, row] = jnp.where(lower, acts[1], acts[0])
    blocks = [
        jnp.concatenate([*grads[h], pack_rows(grads[1 - h], (0, LANES - SZ)[h])], axis=0)
        for h in range(2)
    ]
    for k in range(out_ref.shape[0]):
        out_ref[k] = blocks[OVER_CI_SP[k] % 2]


def backward(
    side_ref, core_ref, gathered_ref, weight_ref, mine_ref, other_ref, spread_ref, taps_ref,
):
    slots, rows, width_in, _ = mine_ref.shape
    rows_y = 2 * slots * rows
    width_out = weight_ref.shape[1]
    core = core_ref[0]
    blank = jnp.zeros(spread_ref.shape[1:], BF16)
    spread_ref[0] = blank
    spread_ref[rows_y + 1] = blank

    for c in range(3):
        block = jnp.concatenate([weight_ref[26 - 3 * ab - c] for ab in range(9)], axis=0)
        taps_ref[c * width_in : (c + 1) * width_in] = block.T
    taps = taps_ref[...]
    side = side_ref[0]
    half, at = width_out // 2, lane((width_out, LANES))
    target = (LANES - SZ) * (1 - side)
    done = 0
    for slot in range(2 * slots):
        place = OVER_CI_SP.index(slot)
        packed = gathered_ref[place, 2 * width_out :]
        for row in range(2):
            beside = jnp.concatenate(
                [
                    pltpu.roll(packed, lax.rem(target + 2 * LANES - SZ * (2 * h + row), LANES), 1)
                    for h in range(2)
                ],
                axis=0,
            )
            zero = jnp.zeros_like(beside)
            own = gathered_ref[place, row * width_out : (row + 1) * width_out]
            seen = (
                jnp.where(
                    at < SZ, jnp.where(side == 1, beside, zero), pltpu.roll(own, SZ, 1)
                ),
                own,
                jnp.where(
                    at >= LANES - SZ,
                    jnp.where(side == 0, beside, zero),
                    pltpu.roll(own, LANES - SZ, 1),
                ),
            )
            for b in range(3):
                spread_ref[2 * slot + row + 1, b * width_out : (b + 1) * width_out] = seen[b]
        while 4 * done + 4 < 2 * slot + 2 or (slot == 2 * slots - 1 and done < slots):
            pairs = [correlate_rows(taps, spread_ref, 4 * done + 2 * k, width_in) for k in range(2)]
            for k in range(rows):
                owner = OVER_CO.index(done)
                mine_ref[owner, k] = jnp.where(core == 0, pairs[0][k], pairs[1][k])
                other_ref[owner, k] = jnp.where(core == 0, pairs[1][k], pairs[0][k])
            done += 1


def add_pair(mine_ref, other_ref, out_ref):
    out_ref[...] = (mine_ref[...].astype(F32) + other_ref[...].astype(F32)).astype(BF16)


def filter_gradient(features_ref, spread_ref, act_ref, out_ref, grad_ref, rows_ref):
    rows_y, width_in, _ = features_ref.shape
    third = spread_ref.shape[1]
    width = third // 3
    z = lane((third, LANES)) % SZ
    zero = jnp.zeros((third, LANES), BF16)
    for y in range(rows_y):
        own = spread_ref[y + 1]
        moved = (
            jnp.where(z == SZ - 1, zero, pltpu.roll(own, LANES - 1, 1)),
            own,
            jnp.where(z == 0, zero, pltpu.roll(own, 1, 1)),
        )
        columns = slice(y * LANES, (y + 1) * LANES)
        for c in range(3):
            grad_ref[c * third : (c + 1) * third, columns] = moved[c]
        for a in range(3):
            source = y + a - 1
            inside = 0 <= source < rows_y
            rows_ref[a * width_in : (a + 1) * width_in, columns] = (
                features_ref[source] if inside else jnp.zeros((width_in, LANES), BF16)
            )
        rows_ref[3 * width_in :, columns] = jnp.ones((16, LANES), BF16)
    total = lax.dot_general(
        grad_ref[...], rows_ref[...], (((1,), (1,)), ((), ())), preferred_element_type=F32
    )
    count = total.shape[0]
    half = count // 2
    out_ref[:count] = total[:, : 2 * width_in]
    last = total[:, 2 * width_in : 3 * width_in]
    out_ref[count : count + half] = jnp.concatenate([last[:half], last[half:]], axis=1)
    start = count + half
    bias = total[third + width : third + 2 * width, 3 * width_in : 3 * width_in + 1]
    out_ref[start : start + width] = jnp.broadcast_to(bias, (width, LANES))
    out_ref[start + width :] = act_ref[1].reshape(2 * width, LANES).astype(F32)


def finish(
    side_ref, shares_ref, own_ref, other_ref, acted_ref, input_ref, weight_ref, bias_ref, act_ref
):
    total = shares_ref[0].astype(F32)
    for k in range(1, shares_ref.shape[0]):
        total = total + shares_ref[k].astype(F32)
    input_ref[...] = total
    side = side_ref[0]
    act_ref[pl.ds(2 * side, 2)] = acted_ref[0]
    received = other_ref[other_ref.shape[0] - 2 * acted_ref.shape[2] :]
    act_ref[pl.ds(2 - 2 * side, 2)] = received.reshape(acted_ref.shape[1:]).astype(BF16)
    _, width_out, width_in = weight_ref.shape
    count = 9 * width_out
    half = count // 2
    both = own_ref[: count + half + width_out] + other_ref[: count + half + width_out]
    for b in range(3):
        for c in range(3):
            start = (3 * c + 2 - b) * width_out
            first = both[start : start + width_out]
            weight_ref[3 * b + c] = first[:, :width_in]
            weight_ref[9 + 3 * b + c] = first[:, width_in:]
            for step in range(0, width_out, 16):
                row = start + step
                if row < half:
                    piece = both[count + row : count + row + 16, :width_in]
                else:
                    piece = both[half + row : half + row + 16, width_in:]
                weight_ref[18 + 3 * b + c, step : step + 16] = piece
    shape = (width_out, width_out)
    diagonal = lax.broadcasted_iota(jnp.int32, shape, 0) == lane(shape)
    sums = both[count + half :, :width_out]
    bias_ref[...] = jnp.sum(jnp.where(diagonal, sums, 0.0), axis=0, keepdims=True)


def local(features, weight, bias_vector, cotangent):
    rows_y, width_in, _ = features.shape
    width_out = weight.shape[2]
    n_ci, n_co = lax.axis_size("ci"), lax.axis_size("co")
    shape = jax.ShapeDtypeStruct
    side = lax.axis_index("sp").astype(jnp.int32).reshape(1)
    core = lax.rem(lax.axis_index("co"), 2).astype(jnp.int32).reshape(1)
    side, core = lax.optimization_barrier((side, core))
    swap = [(0, 1), (1, 0)]
    taps = weight.transpose(0, 2, 1)
    work = 2 * 27 * rows_y * LANES * width_in * width_out
    size = rows_y * LANES * 2

    cotangent_other = lax.ppermute(cotangent, "sp", swap)
    block = (2 * n_ci, 2 * width_out + width_out // 2, LANES)
    partial, bias_columns = call(
        forward,
        (pltpu.VMEM(block, BF16), pltpu.VMEM((width_out, LANES), F32)),
        [SMEM, HBM, HBM, HBM],
        work,
        size * (width_in + width_out),
        [
            pltpu.VMEM(features.shape, BF16),
            pltpu.VMEM(taps.shape, BF16),
            pltpu.VMEM((1, width_out), F32),
            pltpu.VMEM((rows_y + 2, 2 * width_in, LANES), BF16),
            pltpu.VMEM((3 * width_out, 9 * width_in), BF16),
            pltpu.VMEM((3 * width_out, 3 * width_in), BF16),
            pltpu.VMEM((rows_y // 4 + 2, width_in, LANES), BF16),
            pltpu.SemaphoreType.DMA((4,)),
        ],
    )(side, *(stay(x, pltpu.HBM) for x in (features, taps, bias_vector.reshape(1, width_out))))
    both = ("ci", "sp")
    partial, cotangent_other = lax.optimization_barrier((partial, cotangent_other))
    shares = lax.all_to_all(partial, both, 0, 0, tiled=True, axis_index_groups=[OVER_CI_SP])
    acted, copies = call(
        pointwise,
        (pltpu.VMEM((2, 2, width_out, LANES), BF16), pltpu.VMEM(block, BF16)),
        [SMEM, VMEM, VMEM, VMEM, VMEM],
        0,
        2 * size * width_out,
    )(side, shares, bias_columns, cotangent, cotangent_other)
    gathered = lax.all_to_all(copies, both, 0, 0, tiled=True, axis_index_groups=[OVER_CI_SP])
    quarter = (n_co // 2, rows_y // n_co, width_in, LANES)
    mine, other_half, spread = call(
        backward,
        (
            pltpu.VMEM(quarter, BF16),
            pltpu.VMEM(quarter, BF16),
            pltpu.VMEM((rows_y + 2, 3 * width_out, LANES), BF16),
        ),
        [SMEM, SMEM, VMEM, VMEM],
        work,
        size * (width_in + width_out),
        [pltpu.VMEM((3 * width_in, 9 * width_out), BF16)],
    )(side, core, gathered, taps)
    packed = call(
        filter_gradient,
        shape((9 * width_out + 9 * width_out // 2 + 3 * width_out, LANES), F32),
        [VMEM, VMEM, VMEM],
        work,
        size * (width_in + width_out),
        [
            pltpu.VMEM((9 * width_out, rows_y * LANES), BF16),
            pltpu.VMEM((3 * width_in + 16, rows_y * LANES), BF16),
        ],
    )(features, spread, acted)
    received = lax.ppermute(other_half, "co", [(k, k ^ 1) for k in range(n_co)])
    received, packed = lax.optimization_barrier((received, packed))
    summed = call(
        add_pair, pltpu.VMEM(quarter, BF16), [VMEM, VMEM], 0, size * width_in
    )(mine, received)
    same_core = [[2 * k + core_at for k in OVER_CO] for core_at in range(2)]
    shares = lax.all_to_all(summed, "co", 0, 0, tiled=True, axis_index_groups=same_core)
    other = lax.ppermute(packed, "sp", swap)
    input_grad, weight_grad, bias_grad, activated = call(
        finish,
        (
            shape(quarter[1:], F32),
            shape((27, width_out, width_in), F32),
            shape((1, width_out), F32),
            shape(cotangent.shape, BF16),
        ),
        [SMEM] + [VMEM] * 4,
        0,
        27 * 4 * width_in * width_out,
    )(side, shares, packed, other, acted)
    return (activated, input_grad, weight_grad.transpose(0, 2, 1), bias_grad.reshape(width_out))


def solution(mesh):
    placed = (P(None, "ci", "sp"), P(None, "ci", "co"), P("co"), P("ci", "co", "sp"))
    return jax.shard_map(
        local,
        mesh=mesh,
        in_specs=placed,
        out_specs=(P("ci", "co", "sp"), P("co", "ci", "sp"), P(None, "ci", "co"), P("co")),
        check_vma=False,
    )
```

```python
import jax
import jax.numpy as jnp
from jax import lax
from jax.experimental import pallas as pl
from jax.experimental.pallas import tpu as pltpu
from jax.sharding import PartitionSpec as P

SZ = 32
LANES = 128
BF16 = jnp.bfloat16
F32 = jnp.float32
OVER_CI_SP = [0, 14, 12, 10, 8, 6, 4, 2, 1, 15, 13, 11, 9, 7, 5, 3]
OVER_CO = [0, 4, 1, 5, 2, 6, 3, 7]
VMEM = pl.BlockSpec(memory_space=pltpu.VMEM)
SMEM = pl.BlockSpec(memory_space=pltpu.SMEM)
HBM = pl.BlockSpec(memory_space=pltpu.HBM)
stay = pltpu.with_memory_space_constraint


def call(body, outs, specs, flops, moved, scratch=(), vmem=40):
    return pl.pallas_call(
        body,
        out_shape=outs,
        in_specs=specs,
        out_specs=jax.tree.map(lambda _: VMEM, outs),
        scratch_shapes=list(scratch),
        cost_estimate=pl.CostEstimate(flops=flops, bytes_accessed=moved, transcendentals=0),
        compiler_params=pltpu.CompilerParams(vmem_limit_bytes=vmem * 2**20),
    )


def lane(shape):
    return lax.broadcasted_iota(jnp.int32, shape, len(shape) - 1)


def pack_plane(side, planes):
    packed = None
    at = lane(planes[0].shape)
    for k, plane in enumerate(planes):
        moved = pltpu.roll(plane, lax.rem(SZ * k + SZ * (1 - side), LANES), 1)
        packed = moved if packed is None else jnp.where(at >= SZ * k, moved, packed)
    return packed


def neighbours(own):
    at = lane(own.shape)
    zero = jnp.zeros_like(own)
    before = jnp.where(at < SZ, zero, pltpu.roll(own, SZ, 1))
    after = jnp.where(at >= LANES - SZ, zero, pltpu.roll(own, LANES - SZ, 1))
    return before, own, after


def unpack_row(packed, row, target):
    half = LANES // 2
    return jnp.concatenate(
        [pltpu.roll(packed, (target - h * half - SZ * row) % LANES, 1) for h in range(2)], axis=0
    )


def pack_rows(rows, source):
    half = rows[0].shape[0] // 2
    at = lane((half, LANES))
    packed = None
    for k in range(4):
        h, row = divmod(k, 2)
        piece = rows[row][h * half : (h + 1) * half]
        moved = pltpu.roll(piece, lax.rem(SZ * k - source + LANES, LANES), 1)
        packed = moved if k == 0 else jnp.where(at >= SZ * k, moved, packed)
    return packed


def along_z(terms):
    lower, middle, upper = terms
    width = middle.shape[1]
    z = lane((middle.shape[0], LANES)) % SZ
    parts = []
    for start in range(0, width, LANES):
        cut = slice(start, start + LANES)
        parts.append(
            middle[:, cut]
            + jnp.where(z == 0, 0.0, pltpu.roll(lower[:, cut], 1, 1))
            + jnp.where(z == SZ - 1, 0.0, pltpu.roll(upper[:, cut], LANES - 1, 1))
        )
    return parts


def correlate_rows(taps, spread_ref, y, width, own_ref=None):
    def row(at):
        rows = spread_ref[at]
        if own_ref is None:
            return [rows]
        inside = 1 <= at <= own_ref.shape[0]
        own = own_ref[at - 1] if inside else jnp.zeros(own_ref.shape[1:], BF16)
        return [rows[: own.shape[0]], own, rows[own.shape[0] :]]

    columns = jnp.concatenate(
        [jnp.concatenate(sum((row(y + k + a) for a in range(3)), []), axis=0) for k in range(2)],
        axis=1,
    )
    product = jnp.dot(taps, columns, preferred_element_type=F32)
    parts = along_z([product[c * width : (c + 1) * width] for c in range(3)])
    return [part.astype(BF16) for part in parts]


def forward(
    side_ref, core_ref, features_hbm, weight_hbm, bias_hbm, out_ref, column_ref, flipped_ref,
    features_ref, weight_ref, bias_ref, spread_ref, taps_ref, edge_taps_ref, edge_ref, sems,
):
    rows_y, width_in, _ = features_ref.shape
    width_out = weight_ref.shape[1]
    groups = rows_y // 4
    fetch_weight = pltpu.make_async_copy(weight_hbm, weight_ref, sems.at[0])
    step = rows_y // 2
    fetch = [
        pltpu.make_async_copy(
            features_hbm.at[pl.ds(k * step, step)],
            features_ref.at[pl.ds(k * step, step)],
            sems.at[2 + k],
        )
        for k in range(2)
    ]
    fetch_bias = pltpu.make_async_copy(bias_hbm, bias_ref, sems.at[1])
    fetch_weight.start()
    for copy in fetch:
        copy.start()
    fetch_bias.start()
    side = side_ref[0]
    blank = jnp.zeros(spread_ref.shape[1:], BF16)
    spread_ref[0] = blank
    spread_ref[rows_y + 1] = blank
    fetch_weight.wait()
    for c in range(3):
        rows = slice(c * width_out, (c + 1) * width_out)
        taps_ref[rows] = jnp.concatenate([weight_ref[3 * ab + c] for ab in range(9)], axis=1)
        edge_taps_ref[rows] = jnp.concatenate(
            [weight_ref[9 * a + c + 6 * side] for a in range(3)], axis=1
        )
    @pl.when(core_ref[0] == 0)
    def _():
        flip_taps(weight_ref, flipped_ref)

    taps = taps_ref[...]
    fetch_bias.wait()
    shape = (width_out, width_out)
    diagonal = lax.broadcasted_iota(jnp.int32, shape, 0) == lane(shape)
    column = jnp.sum(jnp.where(diagonal, bias_ref[...], 0.0), axis=1, keepdims=True)
    column_ref[...] = jnp.broadcast_to(column, column_ref.shape)
    for copy in fetch:
        copy.wait()
    done = 0
    for group in range(groups):
        planes = [features_ref[4 * group + k] for k in range(4)]
        for k in range(4):
            seen = neighbours(planes[k])
            for b in (0, 2):
                spread_ref[4 * group + k + 1, b // 2 * width_in : (b // 2 + 1) * width_in] = seen[b]
        edge_ref[group + 1] = pack_plane(side, planes)
        while done + 2 < 4 * group or (group == groups - 1 and done < rows_y):
            parts = correlate_rows(taps, spread_ref, done, width_out, features_ref)
            for k in range(2):
                place = OVER_CI_SP.index(done // 2)
                out_ref[place, k * width_out : (k + 1) * width_out] = parts[k]
            done += 2
    none = jnp.zeros(edge_ref.shape[1:], BF16)
    edge_ref[0] = none
    edge_ref[groups + 1] = none
    at = lane((width_in, LANES))
    columns = []
    for group in range(groups):
        last, here, following = (edge_ref[group + k] for k in range(3))
        above = jnp.where(at < SZ, pltpu.roll(last, SZ, 1), pltpu.roll(here, SZ, 1))
        below = jnp.where(
            at >= LANES - SZ,
            pltpu.roll(following, LANES - SZ, 1),
            pltpu.roll(here, LANES - SZ, 1),
        )
        columns.append(jnp.concatenate([above, here, below], axis=0))
    product = jnp.dot(
        edge_taps_ref[...], jnp.concatenate(columns, axis=1), preferred_element_type=F32
    )
    parts = along_z([product[c * width_out : (c + 1) * width_out] for c in range(3)])
    half = width_out // 2
    low = lane((half, LANES)) < LANES // 2
    for group in range(groups):
        here = parts[group]
        turned = pltpu.roll(here, LANES // 2, 1)
        first = jnp.where(low, here[:half], turned[half:])
        second = jnp.where(low, turned[:half], here[half:])
        for k, part in enumerate((first, second)):
            place = OVER_CI_SP.index(2 * group + k)
            out_ref[place, 2 * width_out :] = part.astype(BF16)


def bend(pre):
    return jnp.tanh(0.7978845608 * (pre + 0.044715 * (pre * pre * pre)))


def gelu(pre, cotangent):
    bent = bend(pre)
    half = 0.5 * (1.0 + bent)
    inner = 0.7978845608 * (1.0 + 3.0 * 0.044715 * (pre * pre))
    slope = half + 0.5 * pre * (1.0 - bent * bent) * inner
    return (pre * half).astype(BF16), (cotangent.astype(F32) * slope).astype(BF16)


def pointwise(side_ref, shares_ref, bias_ref, own_ref, other_ref, act_ref, out_ref):
    width = own_ref.shape[1]
    lower, upper = side_ref[0] == 0, side_ref[0] == 1
    bias = bias_ref[...]
    sums = []
    for h in range(2):
        places = [k for k, owner in enumerate(OVER_CI_SP) if owner % 2 == h]
        total = shares_ref[places[0]].astype(F32)
        for k in places[1:]:
            total = total + shares_ref[k].astype(F32)
        sums.append(total)
    at = lane((width, LANES))
    edges = (at >= LANES - SZ, at < SZ)
    grads = ([], [])
    for row in range(2):
        mine = own_ref[2 * side_ref[0] + row]
        theirs = other_ref[2 * side_ref[0] + row]
        cotangents = (jnp.where(lower, mine, theirs), jnp.where(upper, mine, theirs))
        acts = []
        for h in range(2):
            added = unpack_row(sums[1 - h][2 * width :], row, (LANES - SZ, 0)[h])
            pre = sums[h][row * width : (row + 1) * width]
            pre = pre + jnp.where(edges[h], added, 0.0) + bias
            act, grad = gelu(pre, cotangents[h])
            acts.append(act)
            grads[h].append(grad)
        act_ref[0, row] = jnp.where(lower, acts[0], acts[1])
        act_ref[1, row] = jnp.where(lower, acts[1], acts[0])
    blocks = [
        jnp.concatenate([*grads[h], pack_rows(grads[1 - h], (0, LANES - SZ)[h])], axis=0)
        for h in range(2)
    ]
    for k in range(out_ref.shape[0]):
        out_ref[k] = blocks[OVER_CI_SP[k] % 2]


def flip_taps(weight_ref, taps_ref):
    width_in = weight_ref.shape[2]
    for c in range(3):
        block = jnp.concatenate([weight_ref[26 - 3 * ab - c] for ab in range(9)], axis=0)
        taps_ref[c * width_in : (c + 1) * width_in] = block.T


def backward(
    side_ref, core_ref, gathered_ref, weight_ref, flipped_ref,
    mine_ref, other_ref, spread_ref, taps_ref,
):
    slots, rows, width_in, _ = mine_ref.shape
    rows_y = 2 * slots * rows
    width_out = weight_ref.shape[1]
    core = core_ref[0]
    blank = jnp.zeros(spread_ref.shape[1:], BF16)
    spread_ref[0] = blank
    spread_ref[rows_y + 1] = blank


    @pl.when(core == 0)
    def _():
        taps_ref[...] = flipped_ref[...]

    @pl.when(core == 1)
    def _():
        flip_taps(weight_ref, taps_ref)

    taps = taps_ref[...]
    side = side_ref[0]
    half, at = width_out // 2, lane((width_out, LANES))
    target = (LANES - SZ) * (1 - side)
    done = 0
    for slot in range(2 * slots):
        place = OVER_CI_SP.index(slot)
        packed = gathered_ref[place, 2 * width_out :]
        for row in range(2):
            beside = jnp.concatenate(
                [
                    pltpu.roll(packed, lax.rem(target + 2 * LANES - SZ * (2 * h + row), LANES), 1)
                    for h in range(2)
                ],
                axis=0,
            )
            zero = jnp.zeros_like(beside)
            own = gathered_ref[place, row * width_out : (row + 1) * width_out]
            seen = (
                jnp.where(
                    at < SZ, jnp.where(side == 1, beside, zero), pltpu.roll(own, SZ, 1)
                ),
                own,
                jnp.where(
                    at >= LANES - SZ,
                    jnp.where(side == 0, beside, zero),
                    pltpu.roll(own, LANES - SZ, 1),
                ),
            )
            for b in range(3):
                spread_ref[2 * slot + row + 1, b * width_out : (b + 1) * width_out] = seen[b]
        while 4 * done + 4 < 2 * slot + 2 or (slot == 2 * slots - 1 and done < slots):
            pairs = [correlate_rows(taps, spread_ref, 4 * done + 2 * k, width_in) for k in range(2)]
            for k in range(rows):
                owner = OVER_CO.index(done)
                mine_ref[owner, k] = jnp.where(core == 0, pairs[0][k], pairs[1][k])
                other_ref[owner, k] = jnp.where(core == 0, pairs[1][k], pairs[0][k])
            done += 1


def add_pair(mine_ref, other_ref, out_ref):
    out_ref[...] = (mine_ref[...].astype(F32) + other_ref[...].astype(F32)).astype(BF16)


def filter_gradient(features_ref, spread_ref, act_ref, out_ref, grad_ref, rows_ref):
    rows_y, width_in, _ = features_ref.shape
    third = spread_ref.shape[1]
    width = third // 3
    z = lane((third, LANES)) % SZ
    zero = jnp.zeros((third, LANES), BF16)
    for y in range(rows_y):
        own = spread_ref[y + 1]
        moved = (
            jnp.where(z == SZ - 1, zero, pltpu.roll(own, LANES - 1, 1)),
            own,
            jnp.where(z == 0, zero, pltpu.roll(own, 1, 1)),
        )
        columns = slice(y * LANES, (y + 1) * LANES)
        for c in range(3):
            grad_ref[c * third : (c + 1) * third, columns] = moved[c]
        for a in range(3):
            source = y + a - 1
            inside = 0 <= source < rows_y
            rows_ref[a * width_in : (a + 1) * width_in, columns] = (
                features_ref[source] if inside else jnp.zeros((width_in, LANES), BF16)
            )
        rows_ref[3 * width_in :, columns] = jnp.ones((16, LANES), BF16)
    total = lax.dot_general(
        grad_ref[...], rows_ref[...], (((1,), (1,)), ((), ())), preferred_element_type=F32
    )
    count = total.shape[0]
    half = count // 2
    out_ref[:count] = total[:, : 2 * width_in]
    last = total[:, 2 * width_in : 3 * width_in]
    out_ref[count : count + half] = jnp.concatenate([last[:half], last[half:]], axis=1)
    start = count + half
    bias = total[third + width : third + 2 * width, 3 * width_in : 3 * width_in + 1]
    out_ref[start : start + width] = jnp.broadcast_to(bias, (width, LANES))
    out_ref[start + width :] = act_ref[1].reshape(2 * width, LANES).astype(F32)


def finish(
    side_ref, shares_ref, own_ref, other_ref, acted_ref, input_ref, weight_ref, bias_ref, act_ref
):
    total = shares_ref[0].astype(F32)
    for k in range(1, shares_ref.shape[0]):
        total = total + shares_ref[k].astype(F32)
    input_ref[...] = total
    side = side_ref[0]
    act_ref[pl.ds(2 * side, 2)] = acted_ref[0]
    received = other_ref[other_ref.shape[0] - 2 * acted_ref.shape[2] :]
    act_ref[pl.ds(2 - 2 * side, 2)] = received.reshape(acted_ref.shape[1:]).astype(BF16)
    _, width_out, width_in = weight_ref.shape
    count = 9 * width_out
    half = count // 2
    both = own_ref[: count + half + width_out] + other_ref[: count + half + width_out]
    for b in range(3):
        for c in range(3):
            start = (3 * c + 2 - b) * width_out
            first = both[start : start + width_out]
            weight_ref[3 * b + c] = first[:, :width_in]
            weight_ref[9 + 3 * b + c] = first[:, width_in:]
            for step in range(0, width_out, 16):
                row = start + step
                if row < half:
                    piece = both[count + row : count + row + 16, :width_in]
                else:
                    piece = both[half + row : half + row + 16, width_in:]
                weight_ref[18 + 3 * b + c, step : step + 16] = piece
    shape = (width_out, width_out)
    diagonal = lax.broadcasted_iota(jnp.int32, shape, 0) == lane(shape)
    sums = both[count + half :, :width_out]
    bias_ref[...] = jnp.sum(jnp.where(diagonal, sums, 0.0), axis=0, keepdims=True)


def local(features, weight, bias_vector, cotangent):
    rows_y, width_in, _ = features.shape
    width_out = weight.shape[2]
    n_ci, n_co = lax.axis_size("ci"), lax.axis_size("co")
    shape = jax.ShapeDtypeStruct
    side = lax.axis_index("sp").astype(jnp.int32).reshape(1)
    core = lax.rem(lax.axis_index("co"), 2).astype(jnp.int32).reshape(1)
    side, core = lax.optimization_barrier((side, core))
    swap = [(0, 1), (1, 0)]
    taps = weight.transpose(0, 2, 1)
    work = 2 * 27 * rows_y * LANES * width_in * width_out
    size = rows_y * LANES * 2

    cotangent_other = lax.ppermute(cotangent, "sp", swap)
    block = (2 * n_ci, 2 * width_out + width_out // 2, LANES)
    partial, bias_columns, flipped = call(
        forward,
        (
            pltpu.VMEM(block, BF16),
            pltpu.VMEM((width_out, LANES), F32),
            pltpu.VMEM((3 * width_in, 9 * width_out), BF16),
        ),
        [SMEM, SMEM, HBM, HBM, HBM],
        work,
        size * (width_in + width_out),
        [
            pltpu.VMEM(features.shape, BF16),
            pltpu.VMEM(taps.shape, BF16),
            pltpu.VMEM((1, width_out), F32),
            pltpu.VMEM((rows_y + 2, 2 * width_in, LANES), BF16),
            pltpu.VMEM((3 * width_out, 9 * width_in), BF16),
            pltpu.VMEM((3 * width_out, 3 * width_in), BF16),
            pltpu.VMEM((rows_y // 4 + 2, width_in, LANES), BF16),
            pltpu.SemaphoreType.DMA((4,)),
        ],
    )(side, core, *(stay(x, pltpu.HBM) for x in (features, taps, bias_vector.reshape(1, width_out))))
    both = ("ci", "sp")
    partial, cotangent_other = lax.optimization_barrier((partial, cotangent_other))
    shares = lax.all_to_all(partial, both, 0, 0, tiled=True, axis_index_groups=[OVER_CI_SP])
    acted, copies = call(
        pointwise,
        (pltpu.VMEM((2, 2, width_out, LANES), BF16), pltpu.VMEM(block, BF16)),
        [SMEM, VMEM, VMEM, VMEM, VMEM],
        0,
        2 * size * width_out,
    )(side, shares, bias_columns, cotangent, cotangent_other)
    gathered = lax.all_to_all(copies, both, 0, 0, tiled=True, axis_index_groups=[OVER_CI_SP])
    quarter = (n_co // 2, rows_y // n_co, width_in, LANES)
    mine, other_half, spread = call(
        backward,
        (
            pltpu.VMEM(quarter, BF16),
            pltpu.VMEM(quarter, BF16),
            pltpu.VMEM((rows_y + 2, 3 * width_out, LANES), BF16),
        ),
        [SMEM, SMEM, VMEM, VMEM, VMEM],
        work,
        size * (width_in + width_out),
        [pltpu.VMEM((3 * width_in, 9 * width_out), BF16)],
    )(side, core, gathered, taps, flipped)
    packed = call(
        filter_gradient,
        shape((9 * width_out + 9 * width_out // 2 + 3 * width_out, LANES), F32),
        [VMEM, VMEM, VMEM],
        work,
        size * (width_in + width_out),
        [
            pltpu.VMEM((9 * width_out, rows_y * LANES), BF16),
            pltpu.VMEM((3 * width_in + 16, rows_y * LANES), BF16),
        ],
    )(features, spread, acted)
    received = lax.ppermute(other_half, "co", [(k, k ^ 1) for k in range(n_co)])
    received, packed = lax.optimization_barrier((received, packed))
    summed = call(
        add_pair, pltpu.VMEM(quarter, BF16), [VMEM, VMEM], 0, size * width_in
    )(mine, received)
    same_core = [[2 * k + core_at for k in OVER_CO] for core_at in range(2)]
    shares = lax.all_to_all(summed, "co", 0, 0, tiled=True, axis_index_groups=same_core)
    other = lax.ppermute(packed, "sp", swap)
    input_grad, weight_grad, bias_grad, activated = call(
        finish,
        (
            shape(quarter[1:], F32),
            shape((27, width_out, width_in), F32),
            shape((1, width_out), F32),
            shape(cotangent.shape, BF16),
        ),
        [SMEM] + [VMEM] * 4,
        0,
        27 * 4 * width_in * width_out,
    )(side, shares, packed, other, acted)
    return (activated, input_grad, weight_grad.transpose(0, 2, 1), bias_grad.reshape(width_out))


def solution(mesh):
    placed = (P(None, "ci", "sp"), P(None, "ci", "co"), P("co"), P("ci", "co", "sp"))
    return jax.shard_map(
        local,
        mesh=mesh,
        in_specs=placed,
        out_specs=(P("ci", "co", "sp"), P("co", "ci", "sp"), P(None, "ci", "co"), P("co")),
        check_vma=False,
    )
```
